32 devices in a mesh: band: 16 (over z, x, core), grp: 2 (over y).
Axes of the slice: x: 2, y: 2, z: 4, core: 2. Of those that a mesh axis runs over, the one named last changes fastest.
Arguments:
- tokens: bfloat16 [4, 2048, 1024], P('grp', 'band'), may hold values from -6 to 6
- lead_index: int32 [4, 2], P('grp'), may hold values from 1 to 40
- segment: int32 [4, 2048], P('grp'), may hold values from 0 to 1, as said below
- valid: int32 [4, 2048], P('grp'), may hold values from 0 to 1, as said below
- lead_weight: float32 [1024], replicated, may hold values from -4 to 4
- lead_bias: float32 [1024], replicated, may hold values from -6 to 6
- first_gain: float32 [1024], replicated, may hold values from 0.5 to 1.5
- first_shift: float32 [1024], replicated, may hold values from -6 to 6
- heads_weight: bfloat16 [1024, 3072], replicated, may hold values from -0.25 to 0.25
- query_bias: float32 [1024], replicated, may hold values from -6 to 6
- value_bias: float32 [1024], replicated, may hold values from -6 to 6
- output_weight: bfloat16 [1024, 1024], replicated, may hold values from -1.5 to 1.5
- output_bias: float32 [1024], replicated, may hold values from -6 to 6
- second_gain: float32 [1024], replicated, may hold values from 0.5 to 1.5
- second_shift: float32 [1024], replicated, may hold values from -6 to 6
- up_weight: bfloat16 [1024, 4096], replicated, may hold values from -0.1875 to 0.1875
- up_bias: float32 [4096], replicated, may hold values from -6 to 6
- down_weight: bfloat16 [4096, 1024], replicated, may hold values from -0.125 to 0.125
- down_bias: float32 [1024], replicated, may hold values from -6 to 6
- cotangent: bfloat16 [4, 2048, 1024], P('grp', 'band'), may hold values from -6 to 6
Outputs:
- result: bfloat16 [4, 2048, 1024], P('grp', 'band')
- grad_tokens: float32 [4, 2048, 1024], P('grp', 'band')
- grad_lead_weight: float32 [1024], P('band')
- grad_lead_bias: float32 [1024], P('band')
- grad_first_gain: float32 [1024], P('band')
- grad_first_shift: float32 [1024], P('band')
- grad_heads_weight: float32 [1024, 3072], P('band')
- grad_query_bias: float32 [1024], P('band')
- grad_value_bias: float32 [1024], P('band')
- grad_output_weight: float32 [1024, 1024], P('band')
- grad_output_bias: float32 [1024], P('band')
- grad_second_gain: float32 [1024], P('band')
- grad_second_shift: float32 [1024], P('band')
- grad_up_weight: float32 [1024, 4096], P('band')
- grad_up_bias: float32 [4096], P('band')
- grad_down_weight: float32 [4096, 1024], P('band')
- grad_down_bias: float32 [1024], P('band')
The draws below stay inside these ranges and needn't reach their ends.
Inputs may be any that keep to these rules, and one draw needn't show every extreme that they name: `segment`: A group holds one sample (all rows 0) or two; in a two-sample group, within each aligned run of 128 rows the first half is sample 0 and the second half sample 1. Half of the groups hold two samples. Padding lies at the end of a sample's rows within each aligned run of 128 rows, at most 16 rows there; the first row of a sample in each run is valid. `lead_index`: the second entry of a group is read only where the group holds two samples.
All inputs are finite; a program needn't handle non-finite values.
Results may differ from the reference program's by a relative error of at most 0.02.
Values may be sent and summed in bfloat16 or wider, within the bound.
A program may use at most 320 MiB of HBM per device.

```python
import jax
import jax.numpy as jnp
from jax import lax

D = 1024
FF = 4096
HEADS = 16
HEAD_DIM = 64
ROWS_BAND = 128
GROUP_ROWS = 2048
GROUPS = 4


def group_pairs(key):
    order = jax.random.permutation(key, GROUPS)
    return (order % 2).astype(jnp.int32)


def draw_segment(key, part):
    pairs = group_pairs(key)
    where_in = jnp.arange(GROUP_ROWS, dtype=jnp.int32) % ROWS_BAND
    second = (where_in >= ROWS_BAND // 2).astype(jnp.int32)
    return pairs[:, None] * second[None, :]


def draw_valid(key, part):
    pairs = group_pairs(key)
    key = jax.random.fold_in(key, 23)
    runs = GROUP_ROWS // ROWS_BAND
    half = ROWS_BAND // 2
    cuts = jax.random.randint(key, (GROUPS, runs, 2), 0, ROWS_BAND // 8 + 1).astype(jnp.int32)
    position = jnp.arange(ROWS_BAND, dtype=jnp.int32)[None, None, :]
    second = (position >= half).astype(jnp.int32)
    paired = pairs[:, None, None]
    inner = position - paired * second * half
    length = jnp.where(paired == 1, half, ROWS_BAND)
    chosen = jnp.where(paired * second == 1, cuts[:, :, 1:2], cuts[:, :, 0:1])
    marks = (inner < length - chosen).astype(jnp.int32)
    return marks.reshape(GROUPS, GROUP_ROWS)


def touch_ends(entries, own_key, smallest, largest):
    dims = entries.shape
    index_at = [jax.random.randint(jax.random.fold_in(own_key, axis), (), 0, dims[axis]) for axis in range(len(dims))]
    entries = entries.at[tuple(index_at)].set(smallest)
    longest = dims.index(max(dims))
    index_at[longest] = (index_at[longest] + 1) % dims[longest]
    return entries.at[tuple(index_at)].set(largest)


def block_levels(stream_key, shape, cuts, smallest, top_value):
    loudness = 1.0
    for dim, parts in cuts:
        steps = jax.random.uniform(jax.random.fold_in(jax.random.fold_in(stream_key, 6), dim), (parts,), jnp.float32, smallest / len(cuts), top_value / len(cuts))
        loudness = loudness * jnp.repeat(jnp.exp(steps), shape[dim] // parts).reshape((-1,) + (1,) * (len(shape) - 1 - dim))
    return loudness


def bell_draw(rng, shape, deviation, most, pieces=(), held_as=jnp.bfloat16):
    values = deviation * jax.random.normal(rng, shape, jnp.float32)
    if pieces:
        values = values * block_levels(rng, shape, pieces, -0.22, 0.18)
    return jnp.clip(values, -most, most).astype(held_as)


def setup_inputs(seed: int = 0) -> dict:
    splits = jax.random.split(jax.random.key(seed), 21)
    tokens = bell_draw(splits[0], (GROUPS, GROUP_ROWS, D), 1.0, 6.0, ((0, 2), (1, 16)))
    lead_index = touch_ends(jax.random.randint(splits[1], (GROUPS, 2), 1, 41), jax.random.fold_in(splits[1], 1), 1, 40).astype(jnp.int32)
    segment = draw_segment(jax.random.fold_in(splits[20], 71), 0)
    valid = draw_valid(jax.random.fold_in(splits[20], 71), 0)
    lead_weight = bell_draw(splits[4], (D,), 0.3, 4.0, (), jnp.float32)
    lead_bias = bell_draw(splits[5], (D,), 0.5, 6.0, (), jnp.float32)
    first_gain = jnp.clip(1.0 + 0.1 * jax.random.normal(splits[6], (D,), jnp.float32), 0.5, 1.5)
    first_shift = bell_draw(splits[7], (D,), 0.5, 6.0, (), jnp.float32)
    heads_weight = bell_draw(splits[8], (D, 3 * D), (D // 2) ** -0.5, 0.25)
    query_bias = bell_draw(splits[9], (D,), 0.5, 6.0, (), jnp.float32)
    value_bias = bell_draw(splits[10], (D,), 0.5, 6.0, (), jnp.float32)
    output_weight = bell_draw(splits[11], (D, D), (max(D // 64, 1)) ** -0.5, 1.5)
    output_bias = bell_draw(splits[12], (D,), 0.5, 6.0, (), jnp.float32)
    second_gain = jnp.clip(1.0 + 0.1 * jax.random.normal(splits[13], (D,), jnp.float32), 0.5, 1.5)
    second_shift = bell_draw(splits[14], (D,), 0.5, 6.0, (), jnp.float32)
    up_weight = bell_draw(splits[15], (D, FF), D ** -0.5, 0.1875)
    up_bias = bell_draw(splits[16], (FF,), 0.5, 6.0, (), jnp.float32)
    down_weight = bell_draw(splits[17], (FF, D), (FF // 2) ** -0.5, 0.125)
    down_bias = bell_draw(splits[18], (D,), 0.5, 6.0, (), jnp.float32)
    cotangent = bell_draw(splits[19], (GROUPS, GROUP_ROWS, D), 1.0, 6.0, ((0, 2), (1, 16)))
    return {"tokens": tokens, "lead_index": lead_index, "segment": segment, "valid": valid, "lead_weight": lead_weight, "lead_bias": lead_bias, "first_gain": first_gain, "first_shift": first_shift, "heads_weight": heads_weight, "query_bias": query_bias, "value_bias": value_bias, "output_weight": output_weight, "output_bias": output_bias, "second_gain": second_gain, "second_shift": second_shift, "up_weight": up_weight, "up_bias": up_bias, "down_weight": down_weight, "down_bias": down_bias, "cotangent": cotangent}


@jax.custom_vjp
def low(v):
    return lax.optimization_barrier(v.astype(jnp.bfloat16)).astype(jnp.float32)

@jax.custom_vjp
def low_back(v):
    return v

def low_keep(v):
    return (low(v), None)

def low_pass(kept, grad):
    return (grad,)

def back_keep(v):
    return (v, None)

def back_low(kept, grad):
    return (low(grad),)
low.defvjp(low_keep, low_pass)
low_back.defvjp(back_keep, back_low)

def matmul(left, right):
    return jnp.dot(left, right, precision=lax.Precision.HIGHEST, preferred_element_type=jnp.float32)

def layer_norm(values, gain, shift):
    center = values - lax.optimization_barrier(jnp.mean(values, -1, keepdims=True))
    spread = lax.optimization_barrier(jnp.mean(center * center, -1, keepdims=True))
    return center * lax.rsqrt(spread + 1e-05) * gain + shift

def reference(tokens, lead_index, segment, valid, lead_weight, lead_bias, first_gain, first_shift, heads_weight, query_bias, value_bias, output_weight, output_bias, second_gain, second_shift, up_weight, up_bias, down_weight, down_bias, cotangent):
    width = tokens.shape[2]
    group_rows = tokens.shape[1]
    block = min(512, group_rows)
    blocks = group_rows // block
    scale = HEAD_DIM ** (-0.5)
    lead_days = lead_index.astype(jnp.float32) * 0.25
    lead_rows = jnp.where(segment == 0, lead_days[:, 0:1], lead_days[:, 1:2])
    params = (lead_weight, lead_bias, first_gain, first_shift, heads_weight.astype(jnp.float32), query_bias, value_bias, output_weight.astype(jnp.float32), output_bias, second_gain, second_shift, up_weight.astype(jnp.float32), up_bias, down_weight.astype(jnp.float32), down_bias)

    def forward(inputs, weights):
        lead_weight, lead_bias, first_gain, first_shift, heads_weight, query_bias, value_bias, output_weight, output_bias, second_gain, second_shift, up_weight, up_bias, down_weight, down_bias = weights

        def group_layer(items):
            rows_in, lead_row, seg_row, valid_row = items
            start = rows_in + lead_row[:, None] * lead_weight + lead_bias
            first = low(layer_norm(start, first_gain, first_shift))
            joined = matmul(first, heads_weight) + jnp.concatenate([query_bias, jnp.zeros_like(query_bias), value_bias])
            query = low(low_back(joined[:, :width])).reshape(group_rows, HEADS, HEAD_DIM)
            keyset = low(low_back(joined[:, width:2 * width])).reshape(group_rows, HEADS, HEAD_DIM)
            valueset = low(low_back(joined[:, 2 * width:])).reshape(group_rows, HEADS, HEAD_DIM)

            def query_block(piece):
                block_query, block_seg = piece
                scores = low_back(jnp.einsum('qhd,khd->hqk', block_query, keyset, precision=lax.Precision.HIGHEST) * scale)
                allowed = (block_seg[:, None] == seg_row[None, :]) & (valid_row[None, :] == 1)
                scores = jnp.where(allowed[None], scores, -1e+30)
                shifted = jnp.exp(scores - lax.optimization_barrier(jnp.max(scores, -1, keepdims=True)))
                probs = shifted / lax.optimization_barrier(jnp.sum(shifted, -1, keepdims=True))
                return jnp.einsum('hqk,khd->qhd', low(probs), valueset, precision=lax.Precision.HIGHEST)
            mixed = lax.map(jax.checkpoint(query_block), (query.reshape(blocks, block, HEADS, HEAD_DIM), seg_row.reshape(blocks, block)))
            attended = low(low_back(mixed.reshape(group_rows, width)))
            middle = start + low_back(matmul(attended, output_weight) + output_bias)
            second = low(layer_norm(middle, second_gain, second_shift))
            upper = low_back(matmul(second, up_weight) + up_bias)
            hidden = low(jax.nn.gelu(upper, approximate=False))
            return middle + low_back(matmul(hidden, down_weight) + down_bias)
        return lax.map(jax.checkpoint(group_layer), (inputs, lead_rows, segment, valid))
    outcome, backward = jax.vjp(forward, tokens.astype(jnp.float32), params)
    grad_tokens, grads = backward(cotangent.astype(jnp.float32))
    return (outcome.astype(jnp.bfloat16), grad_tokens, grads[0], grads[1], grads[2], grads[3], grads[4], grads[5], grads[6], grads[7], grads[8], grads[9], grads[10], grads[11], grads[12], grads[13], grads[14])
```

```python
import functools

import jax
import jax.numpy as jnp
from jax import lax
from jax.experimental import pallas as pl
from jax.experimental.pallas import tpu as pltpu
from jax.sharding import PartitionSpec as P

HEADS = 16
HEAD_DIM = 64
LANES = 128
MESH = pl.DeviceIdType.MESH
F32 = jnp.float32
BF16 = jnp.bfloat16
VMEM_BYTES = 56 * 2**20
MASKED = -1e30


def layer_norm(values, gain, shift):
    center = values - jnp.mean(values, -1, keepdims=True)
    spread = jnp.mean(center * center, -1, keepdims=True)
    return center * lax.rsqrt(spread + 1e-05) * gain + shift


def gelu_exact(values):
    return jax.nn.gelu(values, approximate=False)


def lane_of(shape):
    return lax.broadcasted_iota(jnp.int32, shape, 1)


def in_head(shape, head):
    return lane_of(shape) // HEAD_DIM == head


def spare_lane(shape, head):
    lane = lane_of(shape)
    return jnp.where(lane // HEAD_DIM == head, LANES, lane % HEAD_DIM)


def split_terms(column, spare):
    high = column.astype(BF16).astype(F32)
    middle = (column - high).astype(BF16).astype(F32)
    low = column - high - middle
    return (
        jnp.where(spare == 2, high, 0.0)
        + jnp.where(spare == 3, middle, 0.0)
        + jnp.where(spare == 4, low, 0.0)
    )


def dot_nt(left, right):
    return lax.dot_general(left, right, (((1,), (1,)), ((), ())), preferred_element_type=F32)


def dot_tn(left, right):
    return lax.dot_general(left, right, (((0,), (0,)), ((), ())), preferred_element_type=F32)


def dot_nn(left, right):
    return jnp.dot(left, right, preferred_element_type=F32)


def forward_kernel(
    block, members, pairs,
    blocks_ref, query_aux_ref, key_aux_ref,
    qkv_ref, attended_ref, out_full_ref, query_ref,
    qkv_in, key_s, value_s, out_s,
    local_sem, keep_sem, qkv_send, qkv_recv, out_send, out_recv,
):
    rows = members * block
    scale = HEAD_DIM ** (-0.5)
    copies = members // pairs
    band, grp = lax.axis_index("band"), lax.axis_index("grp")
    me = lax.rem(band, members)
    base = band - me
    others = [lax.rem(me + i, members) for i in range(1, members)]

    barrier = pltpu.get_barrier_semaphore()
    for other in others:
        pl.semaphore_signal(barrier, inc=1, device_id=(base + other, grp), device_id_type=MESH)
    pl.semaphore_wait(barrier, len(others))

    def remote(source, target, send, recv, device):
        return pltpu.make_async_remote_copy(
            src_ref=source, dst_ref=target, send_sem=send, recv_sem=recv, device_id=device, device_id_type=MESH
        )

    qkv_copies = {}
    for t in (1, 2, 0):
        for i, other in enumerate(others):
            qkv_copies[t, i] = remote(
                blocks_ref.at[other // copies, t],
                qkv_in.at[me, t],
                qkv_send.at[t, i],
                qkv_recv.at[t, i],
                (base + other, grp),
            )
            qkv_copies[t, i].start()
    own = pltpu.make_async_copy(blocks_ref.at[me // copies], qkv_in.at[me], local_sem)
    own.start()
    own.wait()
    for i in range(members - 1):
        qkv_copies[1, i].wait_recv()
    keys = qkv_in[:, 1].reshape(rows, LANES)
    for head in range(2):
        key_s[head] = jnp.where(in_head(keys.shape, head), keys, key_aux_ref[...])
    for i in range(members - 1):
        qkv_copies[2, i].wait_recv()
    value_s[...] = qkv_in[:, 2].reshape(rows, LANES)

    def sends_to(other):
        return (lax.rem(other, copies) == lax.rem(me, copies)) & (other != me)

    def out_copy(other):
        return remote(
            out_s.at[other],
            attended_ref.at[me // copies],
            out_send.at[other // copies],
            out_recv.at[me // copies],
            (base + other, grp),
        )

    @pl.loop(0, members)
    def _(i):
        other = lax.rem(me + members - i, members)

        @pl.when(i > 0)
        def _():
            pltpu.make_async_copy(qkv_in.at[other, 0], qkv_in.at[other, 0], qkv_recv.at[0, i - 1]).wait()

        here = pl.ds(pl.multiple_of(other * block, block), block)
        query = qkv_in[other, 0].astype(F32) * scale
        aux = query_aux_ref[here].astype(F32)
        shape = query.shape
        mixed = []
        for head in range(2):
            inside = in_head(shape, head)
            marked = jnp.where(inside, query, aux)
            scores = dot_nt(marked.astype(BF16), key_s[head])
            peak = jnp.max(scores, -1, keepdims=True)
            weights = jnp.exp(scores - peak)
            total = jnp.sum(weights, -1, keepdims=True)
            mixed.append(dot_nn(weights.astype(BF16), value_s[...]) / total)
            logsum = peak + jnp.log(total)
            marked = marked + split_terms(-logsum, spare_lane(shape, head))
            query_ref[head, here] = marked.astype(BF16)
        both = jnp.where(in_head(shape, 0), mixed[0], mixed[1])
        out_full_ref[here] = both
        out_s[other, 0] = both.astype(BF16)

        @pl.when(sends_to(other))
        def _():
            out_copy(other).start()

    keep = pltpu.make_async_copy(qkv_in, qkv_ref, keep_sem)
    keep.start()
    own_out = pltpu.make_async_copy(out_s.at[me], attended_ref.at[me // copies], local_sem)
    own_out.start()
    keep.wait()
    own_out.wait()
    for copy in qkv_copies.values():
        copy.wait_send()
    for other in others:

        @pl.when(sends_to(other))
        def _():
            out_copy(other).wait_send()

    for i in range(1, pairs):
        slot = lax.rem(me // copies + i, pairs)
        pltpu.make_async_copy(attended_ref.at[slot], attended_ref.at[slot], out_recv.at[slot]).wait()


def attention_forward(blocks, query_aux, key_aux, members, collective_id):
    pairs, _, block, _ = blocks.shape
    rows = members * block
    vmem = pl.BlockSpec(memory_space=pltpu.VMEM)
    anywhere = pl.BlockSpec(memory_space=pl.ANY)
    dma = pltpu.SemaphoreType.DMA
    return pl.pallas_call(
        functools.partial(forward_kernel, block, members, pairs),
        out_shape=(
            jax.ShapeDtypeStruct((members, 3, block, LANES), BF16),
            jax.ShapeDtypeStruct((pairs, 1, block, LANES), BF16),
            jax.ShapeDtypeStruct((rows, LANES), F32),
            jax.ShapeDtypeStruct((2, rows, LANES), BF16),
        ),
        in_specs=[anywhere, vmem, vmem],
        out_specs=(anywhere, anywhere, vmem, vmem),
        scratch_shapes=[
            pltpu.VMEM((members, 3, block, LANES), BF16),
            pltpu.VMEM((2, rows, LANES), BF16),
            pltpu.VMEM((rows, LANES), BF16),
            pltpu.VMEM((members, 1, block, LANES), BF16),
            dma, dma, dma((3, members)), dma((3, members)), dma((members,)), dma((members,)),
        ],
        compiler_params=pltpu.CompilerParams(
            vmem_limit_bytes=VMEM_BYTES, collective_id=collective_id, has_side_effects=True
        ),
        cost_estimate=pl.CostEstimate(
            flops=8 * rows * rows * LANES, bytes_accessed=32 * 2**20, transcendentals=2 * rows * rows
        ),
        name="attention_forward",
    )(blocks, query_aux, key_aux)


def device_at(axis, index):
    band, grp = lax.axis_index("band"), lax.axis_index("grp")
    return (index, grp) if axis == "band" else (band, index)


def flip(axis, bit):
    index = lax.axis_index(axis)
    mine = lax.rem(index // (1 << bit), 2)
    return mine, device_at(axis, index + (1 - 2 * mine) * (1 << bit))


def normalised(values):
    center = values - jnp.mean(values, -1, keepdims=True)
    spread = jnp.mean(center * center, -1, keepdims=True)
    inverse = lax.rsqrt(spread + 1e-05)
    return center * inverse, inverse


def norm_backward(grads, gain, unit, inverse):
    inner = grads * gain
    at_input = inverse * (
        inner
        - jnp.mean(inner, -1, keepdims=True)
        - unit * jnp.mean(inner * unit, -1, keepdims=True)
    )
    return at_input, jnp.sum(grads * unit, 0, keepdims=True), jnp.sum(grads, 0, keepdims=True)


def by_core(value, core, held, away_ref, stay_ref):
    split = value.astype(BF16).reshape(-1, 2, held, value.shape[-1])
    even, odd = split[:, 0], split[:, 1]
    away_ref[...] = jnp.where(core == 0, odd, even)
    stay_ref[...] = jnp.where(core == 0, even, odd)


def heads_kernel(
    tokens_ref, lead_ref, lead_weight_ref, lead_bias_ref, gain_ref, shift_ref, weight_ref, bias_ref,
    start_ref, first_ref, out_ref,
):
    part = pl.program_id(0)

    @pl.when(part == 0)
    def _():
        start = tokens_ref[...].astype(F32) + lead_ref[...] * lead_weight_ref[...] + lead_bias_ref[...]
        start_ref[...] = start
        first_ref[...] = (normalised(start)[0] * gain_ref[...] + shift_ref[...]).astype(BF16)

    joined = (dot_nn(first_ref[...], weight_ref[...]) + bias_ref[0]).astype(BF16)
    for pair in range(out_ref.shape[0]):
        out_ref[pair, 0] = joined[:, pair * LANES : (pair + 1) * LANES]


def constant(*shape):
    return pl.BlockSpec(shape, lambda *i: (0,) * len(shape))


def heads_forward(tokens, lead_rows, lead_weight, lead_bias, gain, shift, weight, bias):
    total, width = tokens.shape
    pairs = width // LANES
    row = lambda v: v.reshape(1, width)
    return pl.pallas_call(
        heads_kernel,
        grid=(3,),
        out_shape=(
            jax.ShapeDtypeStruct((total, width), F32),
            jax.ShapeDtypeStruct((total, width), BF16),
            jax.ShapeDtypeStruct((pairs, 3, total, LANES), BF16),
        ),
        in_specs=[constant(total, width), constant(total, 1)]
        + [constant(1, width)] * 4
        + [
            pl.BlockSpec((width, width), lambda i: (0, i)),
            pl.BlockSpec((1, 1, width), lambda i: (i, 0, 0)),
        ],
        out_specs=(
            constant(total, width),
            constant(total, width),
            pl.BlockSpec((pairs, 1, total, LANES), lambda i: (0, i, 0, 0)),
        ),
        compiler_params=pltpu.CompilerParams(vmem_limit_bytes=VMEM_BYTES),
        cost_estimate=pl.CostEstimate(
            flops=6 * total * width * width, bytes_accessed=6 * width * width, transcendentals=0
        ),
        name="heads_forward",
    )(tokens, lead_rows, row(lead_weight), row(lead_bias), row(gain), row(shift), weight, bias)


def feed_kernel(
    core_ref, attended_ref, start_ref, grad_ref, output_weight_ref, output_bias_ref, gain_ref, shift_ref,
    up_ref, up_bias_ref, down_ref, down_bias_ref,
    result_ref, grad_middle_ref, grad_attended_ref, down_away, down_stay, up_away, up_stay,
    output_away, output_stay, vectors_ref, up_vector_ref,
    attended_s, middle_s, unit_s, inverse_s, second_s, second_turned, result_s, grad_second_s,
):
    step, steps = pl.program_id(0), pl.num_programs(0)
    core = core_ref[0]
    pairs = attended_ref.shape[0]

    @pl.when(step == 0)
    def _():
        for pair in range(pairs):
            attended_s[:, pair * LANES : (pair + 1) * LANES] = attended_ref[pair, 0]
        middle = (
            start_ref[...] + dot_nn(attended_s[...], output_weight_ref[...]) + output_bias_ref[...]
        )
        middle_s[...] = middle
        unit, inverse = normalised(middle)
        unit_s[...] = unit
        inverse_s[...] = inverse
        second = unit * gain_ref[...] + shift_ref[...]
        second_s[...] = second.astype(BF16)
        second_turned[...] = second.T.astype(BF16)
        result_s[...] = jnp.zeros_like(result_s)
        grad_second_s[...] = jnp.zeros_like(grad_second_s)

    grads = grad_ref[...]
    upper = dot_nn(second_s[...], up_ref[...]) + up_bias_ref[...]
    level = 0.5 + 0.5 * lax.erf(upper * 0.7071067811865476)
    hidden = (upper * level).astype(BF16)
    slope = level + upper * (0.3989422804014327 * jnp.exp(-0.5 * upper * upper))
    result_s[...] += dot_nn(hidden, down_ref[...])
    by_core(dot_tn(hidden, grads), core, down_away.shape[1], down_away, down_stay)
    grad_upper_wide = dot_nt(grads, down_ref[...]) * slope
    grad_upper = grad_upper_wide.astype(BF16)
    up_vector_ref[...] = jnp.sum(grad_upper.astype(F32), 0, keepdims=True)
    by_core(dot_nn(second_turned[...], grad_upper), core, up_away.shape[1], up_away, up_stay)
    grad_second_s[...] += dot_nt(grad_upper, up_ref[...])

    @pl.when(step == steps - 1)
    def _():
        result_ref[...] = (middle_s[...] + result_s[...] + down_bias_ref[...]).astype(BF16)
        wide = grads.astype(F32)
        at_input, grad_gain, grad_shift = norm_backward(
            grad_second_s[...], gain_ref[...], unit_s[...], inverse_s[...]
        )
        grad_middle = at_input + wide
        grad_middle_ref[...] = grad_middle
        branch = grad_middle.astype(BF16)
        by_core(dot_tn(attended_s[...], branch), core, output_away.shape[1], output_away, output_stay)
        grad_attended = dot_nt(branch, output_weight_ref[...]).astype(BF16)
        for pair in range(pairs):
            grad_attended_ref[pair, 0] = grad_attended[:, pair * LANES : (pair + 1) * LANES]
        vectors_ref[0:1] = jnp.sum(branch.astype(F32), 0, keepdims=True)
        vectors_ref[1:2] = grad_gain
        vectors_ref[2:3] = grad_shift
        vectors_ref[3:4] = jnp.sum(wide, 0, keepdims=True)


def feed(core, attended, start, grads, output_weight, output_bias, gain, shift, up, up_bias, down, down_bias, bands):
    total, width = start.shape
    inner = up.shape[1]
    pairs = width // LANES
    chunk = 512
    held, held_down = width // bands, inner // bands
    per_chunk = chunk // held_down // 2
    row = lambda v: v.reshape(1, -1)
    half = bands // 2
    one = lambda *shape: constant(*shape)
    return pl.pallas_call(
        feed_kernel,
        grid_spec=pltpu.PrefetchScalarGridSpec(
            num_scalar_prefetch=1,
            grid=(inner // chunk,),
            in_specs=[
                one(pairs, 1, total, LANES),
                one(total, width),
                one(total, width),
                one(width, width),
                one(1, width),
                one(1, width),
                one(1, width),
                pl.BlockSpec((width, chunk), lambda j, c: (0, j)),
                pl.BlockSpec((1, chunk), lambda j, c: (0, j)),
                pl.BlockSpec((chunk, width), lambda j, c: (j, 0)),
                one(1, width),
            ],
            out_specs=(
                one(total, width),
                one(total, width),
                one(pairs, 1, total, LANES),
                pl.BlockSpec((per_chunk, held_down, width), lambda j, c: (j, 0, 0)),
                pl.BlockSpec((per_chunk, held_down, width), lambda j, c: (j, 0, 0)),
                pl.BlockSpec((half, held, chunk), lambda j, c: (0, 0, j)),
                pl.BlockSpec((half, held, chunk), lambda j, c: (0, 0, j)),
                one(half, held, width),
                one(half, held, width),
                one(8, width),
                pl.BlockSpec((1, chunk), lambda j, c: (0, j)),
            ),
            scratch_shapes=[
                pltpu.VMEM((total, width), BF16),
                pltpu.VMEM((total, width), F32),
                pltpu.VMEM((total, width), F32),
                pltpu.VMEM((total, 1), F32),
                pltpu.VMEM((total, width), BF16),
                pltpu.VMEM((width, total), BF16),
                pltpu.VMEM((total, width), F32),
                pltpu.VMEM((total, width), F32),
            ],
        ),
        out_shape=(
            jax.ShapeDtypeStruct((total, width), BF16),
            jax.ShapeDtypeStruct((total, width), F32),
            jax.ShapeDtypeStruct((pairs, 1, total, LANES), BF16),
            jax.ShapeDtypeStruct((half, held_down, width), BF16),
            jax.ShapeDtypeStruct((half, held_down, width), BF16),
            jax.ShapeDtypeStruct((half, held, inner), BF16),
            jax.ShapeDtypeStruct((half, held, inner), BF16),
            jax.ShapeDtypeStruct((half, held, width), BF16),
            jax.ShapeDtypeStruct((half, held, width), BF16),
            jax.ShapeDtypeStruct((8, width), F32),
            jax.ShapeDtypeStruct((1, inner), F32),
        ),
        compiler_params=pltpu.CompilerParams(vmem_limit_bytes=VMEM_BYTES),
        cost_estimate=pl.CostEstimate(
            flops=12 * total * width * inner, bytes_accessed=8 * width * inner, transcendentals=2 * total * inner
        ),
        name="feed",
    )(
        core, attended, start, grads, output_weight, row(output_bias), row(gain), row(shift),
        up, row(up_bias), down, row(down_bias),
    )


LINK = 22.3
CORE = 1.5
ADD = 0.35
HOP = 1.5


def plan_events(parts, tasks):
    free, waiting, slots, now = {}, [], [[] for _ in range(len(tasks) + 1)], 0.0
    ready = 3.0
    for k, (size, links) in enumerate(parts):
        ready += size * CORE
        waiting.append((ready, k, size, list(links)))
    for slot in range(len(tasks) + 1):
        while waiting:
            waiting.sort()
            if slot < len(tasks) and waiting[0][0] > now:
                break
            arrival, k, size, links = waiting.pop(0)
            now = max(now, arrival) + size * ADD
            slots[slot].append(k)
            if links:
                link = links.pop(0)
                size /= 2
                begin = max(now, free.get(link, 0.0))
                if link == "Z":
                    end = begin + 2 * size * LINK
                    free["z"] = max(free.get("z", 0.0), now) + size * LINK
                else:
                    end = begin + size * LINK
                free[link] = end
                waiting.append((end + HOP, k, size, links))
            else:
                free["y"] = max(now, free.get("y", 0.0)) + size * LINK
        if slot < len(tasks):
            now += tasks[slot]
    return slots


class Flow:
    def __init__(self, k, plan, away, stay, core_in, stay_s, buffers, sems):
        self.k, self.plan, self.away, self.stay = k, plan, away, stay
        self.core_in, self.stay_s, self.buffers = core_in, stay_s, buffers
        self.core_send, self.core_recv, self.stay_sem, self.send_sem, self.recv_sem = sems
        self.stages, self.lead = plan["stages"], list(plan["lead"])
        self.flips = [flip(*stage) for stage in self.stages]
        self.core_other = flip("band", 0)[1]
        self.held, self.at = None, -1

    @staticmethod
    def shapes(plan):
        shape, lead = [2] * len(plan["lead"]) + [plan["rows"][1], plan["columns"][1]], list(plan["lead"])
        found = [tuple(shape)]
        for axis, bit in plan["stages"]:
            if axis == "band":
                at = lead.index(bit)
                del shape[at], lead[at]
            else:
                shape[-1] //= 2
            found.append(tuple(shape))
        return found

    def region(self, stage, index):
        (first, rows), (column, columns) = self.plan["rows"], self.plan["columns"]
        where = [slice(None)] * len(self.plan["lead"]) + [pl.ds(first, rows), pl.ds(column, columns)]
        if stage is not None:
            axis, bit = stage
            if axis == "band":
                where[self.plan["lead"].index(bit)] = index
            else:
                half = columns // 2
                where[-1] = pl.ds(pl.multiple_of(column + index * half, LANES), half)
        return tuple(where)

    def pick(self, ref, index):
        axis, bit = self.stages[self.at]
        where = [slice(None)] * len(ref.shape)
        if axis == "band":
            where[self.lead.index(bit)] = index
        else:
            half = ref.shape[-1] // 2
            where[-1] = pl.ds(pl.multiple_of(index * half, LANES), half)
        return tuple(where)

    def core_copy(self):
        return pltpu.make_async_remote_copy(
            src_ref=self.away.at[self.region(None, None)],
            dst_ref=self.core_in,
            send_sem=self.core_send.at[self.k],
            recv_sem=self.core_recv.at[self.k],
            device_id=self.core_other,
            device_id_type=MESH,
        )

    def stay_copy(self, index):
        return pltpu.make_async_copy(
            self.stay.at[self.region(self.stages[0], index)], self.stay_s, self.stay_sem.at[self.k]
        )

    def stage_copy(self, stage, source):
        return pltpu.make_async_remote_copy(
            src_ref=source,
            dst_ref=self.buffers[stage],
            send_sem=self.send_sem.at[self.k, stage],
            recv_sem=self.recv_sem.at[self.k, stage],
            device_id=self.flips[stage][1],
            device_id_type=MESH,
        )

    def start(self):
        self.core_copy().start()
        self.stay_copy(1 - self.flips[0][0]).start()

    def advance(self):
        if self.at < 0:
            self.at = 0
            mine = self.flips[0][0]
            self.core_copy().wait_recv()
            self.stay_copy(1 - mine).wait()
            away = self.pick(self.core_in, 1 - mine)
            self.core_in[away] = self.core_in[away] + self.stay_s[...]
            self.stay_copy(mine).start()
            self.held = self.core_in
        else:
            mine = self.flips[self.at][0]
            buffer = self.buffers[self.at]
            self.stage_copy(self.at, buffer).wait_recv()
            kept = self.held[self.pick(self.held, mine)]
            if self.at == 0:
                self.stay_copy(mine).wait()
                kept = kept + self.stay_s[...]
            buffer[...] = buffer[...] + kept
            axis, bit = self.stages[self.at]
            if axis == "band":
                self.lead.remove(bit)
            self.held = buffer
            self.at += 1
        if self.at == len(self.stages):
            return True
        self.stage_copy(self.at, self.held.at[self.pick(self.held, 1 - self.flips[self.at][0])]).start()
        return False

    def drain(self):
        self.core_copy().wait_send()
        for stage, buffer in enumerate(self.buffers):
            self.stage_copy(stage, buffer).wait_send()


class FullFlow:
    def __init__(self, held, stages, buffers, send_sem, recv_sem):
        self.held, self.stages, self.buffers = held, stages, buffers
        self.send_sem, self.recv_sem = send_sem, recv_sem
        self.flips = [flip(*stage) for stage in stages]
        self.at = 0

    def copy(self, stage, source):
        return pltpu.make_async_remote_copy(
            src_ref=source,
            dst_ref=self.buffers[stage],
            send_sem=self.send_sem.at[stage],
            recv_sem=self.recv_sem.at[stage],
            device_id=self.flips[stage][1],
            device_id_type=MESH,
        )

    def send(self):
        if self.at < len(self.stages):
            self.copy(self.at, self.held).start()

    def step(self):
        if self.at < len(self.stages):
            buffer = self.buffers[self.at]
            self.copy(self.at, buffer).wait_recv()
            buffer[...] = buffer[...] + self.held[...]
            self.held = buffer
            self.at += 1
            self.send()

    def drain(self):
        for stage, buffer in enumerate(self.buffers):
            self.copy(stage, buffer).wait_send()


def backward_kernel(
    block, members, pairs, grps, plans, slots, vector_stages,
    grad_ref, qkv_ref, key_aux_ref, query_ref, out_full_ref, first_ref,
    weight_ref, start_ref, grad_middle_ref, gain_ref, lead_ref, feed_ref, up_vector_ref, result_ref, *refs,
):
    count = len(plans)
    arrays = max(plan["array"] for plan in plans) + 1
    refs = list(refs)

    def grab(n):
        found = refs[:n]
        del refs[:n]
        return found

    away_refs, stay_refs = grab(arrays), grab(arrays)
    up_ref, down_ref, output_ref, heads_ref, vectors_ref = grab(5)
    own_tokens_ref, other_tokens_ref, other_result_ref, first_other = grab(4)
    grad_in, grad_s, query_s, plain_s, query_sum, out_s, joined_in = grab(7)
    normed_s, heads_s, heads_in, heads_got, heads_sum = grab(5)
    weight_s, joined_s, tokens_s, vectors_s = grab(4)
    core_in, stay_s = grab(count), grab(count)
    buffers = [grab(len(plan["stages"])) for plan in plans]
    vector_buffers = grab(len(vector_stages))
    grp_count = bits(grps)
    heads_buffers = grab(grp_count)
    (
        local_sem, grad_send, grad_recv, out_send, out_recv, query_send, query_recv, first_send, first_recv,
        normed_sem, weight_sem, swap_send, swap_recv, vector_send, vector_recv, far_send, far_recv,
        heads_send, heads_recv, heads_two_send, heads_two_recv, gather_send, gather_recv, own_sem,
    ) = grab(24)
    flow_sems = grab(5)

    rows = key_aux_ref.shape[0]
    width = start_ref.shape[1]
    scale = HEAD_DIM ** (-0.5)
    copies = members // pairs
    band, grp = lax.axis_index("band"), lax.axis_index("grp")
    me = lax.rem(band, members)
    base = band - me
    others = [lax.rem(me + i, members) for i in range(1, members)]
    groups_off = [lax.rem(grp + i, grps) for i in range(1, grps)]
    half, far = flip("band", bits(members))
    core_other = flip("band", 0)[1]
    flows = [
        Flow(k, plan, away_refs[plan["array"]], stay_refs[plan["array"]], core_in[k], stay_s[k], buffers[k], flow_sems)
        for k, plan in enumerate(plans)
    ]
    vectors = FullFlow(vectors_s, vector_stages, vector_buffers, vector_send, vector_recv)
    heads_flow = FullFlow(
        heads_sum, [("grp", b) for b in range(grp_count)], heads_buffers, heads_two_send, heads_two_recv
    )

    barrier = pltpu.get_barrier_semaphore()
    greeted = [(base + other, grp) for other in others] + [(band, g) for g in groups_off] + [far]
    for device in greeted:
        pl.semaphore_signal(barrier, inc=1, device_id=device, device_id_type=MESH)
    pl.semaphore_wait(barrier, len(greeted))

    def remote(source, target, send, recv, device):
        return pltpu.make_async_remote_copy(
            src_ref=source, dst_ref=target, send_sem=send, recv_sem=recv, device_id=device, device_id_type=MESH
        )

    grad_copies = [
        remote(
            grad_ref.at[other // copies], grad_in.at[me], grad_send.at[i], grad_recv.at[i], (base + other, grp)
        )
        for i, other in enumerate(others)
    ]
    for copy in grad_copies:
        copy.start()
    own = pltpu.make_async_copy(grad_ref.at[me // copies], grad_in.at[me], local_sem)
    own.start()
    for flow in flows:
        flow.start()
    first_copy = remote(first_ref, first_other, first_send, first_recv, core_other)
    first_copy.start()
    result_copy = remote(result_ref.at[1 - half], other_result_ref, swap_send.at[0], swap_recv.at[0], far)

    def weight_load(t):
        return pltpu.make_async_copy(
            weight_ref.at[:, pl.ds(t * width, width)], weight_s.at[t % 2], weight_sem.at[t % 2]
        )

    for t in range(2):
        weight_load(t).start()
    query_s[...] = qkv_ref[:, 0].reshape(rows, LANES)
    query_sum[...] = jnp.zeros_like(query_sum)

    gathers = []

    def gather_copies(k):
        plan, flow = plans[k], flows[k]
        target = (up_ref, down_ref, output_ref)[plan["array"]]
        size = plan["columns"][1]
        columns = size >> grp_count
        offset = plan["columns"][0]
        for b in range(grp_count):
            size //= 2
            offset = offset + flip("grp", b)[0] * size
        where = target.at[pl.ds(*plan["rows"]), pl.ds(pl.multiple_of(offset, LANES), columns)]
        held = flow.buffers[-1]
        mine = pltpu.make_async_copy(held, where, own_sem.at[k])
        return [mine] + [
            remote(held, where, gather_send.at[k, i], gather_recv.at[k, i], (band, g))
            for i, g in enumerate(groups_off)
        ]

    def advance(slot):
        for k in slots[slot]:
            if flows[k].advance():
                for copy in gather_copies(k):
                    copy.start()

    advance(0)
    own.wait()
    for copy in grad_copies:
        copy.wait_recv()
    grads = grad_in[...].reshape(rows, LANES)
    plain_s[...] = grads
    wide = grads.astype(F32)
    product = wide * out_full_ref[...]
    for head in range(2):
        inside = in_head(wide.shape, head)
        delta = jnp.sum(jnp.where(inside, product, 0.0), -1, keepdims=True)
        marked = jnp.where(inside, wide, split_terms(-delta, spare_lane(wide.shape, head)))
        grad_s[head] = marked.astype(BF16)

    def sends_to(other):
        return (lax.rem(other, copies) == lax.rem(me, copies)) & (other != me)

    def out_copy(other):
        return remote(
            out_s.at[other, pl.ds(1, 2)],
            joined_in.at[me // copies, pl.ds(1, 2)],
            out_send.at[other // copies],
            out_recv.at[me // copies],
            (base + other, grp),
        )

    def query_copy(other):
        return remote(
            out_s.at[other, 0],
            joined_in.at[me // copies, 0],
            query_send.at[other // copies],
            query_recv.at[me // copies],
            (base + other, grp),
        )

    sub = min(block, 2**19 // rows)

    @pl.loop(0, members)
    def _(i):
        for slot in range(1, 1 + members):
            if slots[slot]:

                @pl.when(i == slot - 1)
                def _(slot=slot):
                    advance(slot)

        other = lax.rem(me + 1 + i, members)
        for low in range(0, block, sub):
            here = pl.ds(pl.multiple_of(other * block + low, sub), sub)
            key = qkv_ref[other, 1, pl.ds(low, sub)]
            value = qkv_ref[other, 2, pl.ds(low, sub)]
            aux = key_aux_ref[here]
            shape = key.shape
            grad_key, grad_value = [], []
            for head in range(2):
                inside = in_head(shape, head)
                spare = spare_lane(shape, head)
                ones = jnp.where((spare >= 2) & (spare <= 4), 1.0, 0.0).astype(BF16)
                probs = jnp.exp(dot_nt(jnp.where(inside, key, aux), query_ref[head]))
                grad_probs = dot_nt(jnp.where(inside, value, ones), grad_s[head])
                grad_scores = (probs * grad_probs).astype(BF16)
                grad_value.append(dot_nn(probs.astype(BF16), plain_s[...]))
                grad_key.append(dot_nn(grad_scores, query_s[...]))
                query_sum[...] += dot_tn(jnp.where(inside, key, jnp.zeros_like(key)), grad_scores)
            first = in_head(shape, 0)
            out_s[other, 1, pl.ds(low, sub)] = (jnp.where(first, grad_key[0], grad_key[1]) * scale).astype(BF16)
            out_s[other, 2, pl.ds(low, sub)] = jnp.where(first, grad_value[0], grad_value[1]).astype(BF16)

        @pl.when(sends_to(other))
        def _():
            out_copy(other).start()

    slot = members + 1
    advance(slot)
    out_s[:, 0] = (query_sum[...].T * scale).astype(BF16).reshape(members, block, LANES)
    for other in others:

        @pl.when(sends_to(other))
        def _():
            query_copy(other).start()

    joined_in[me // copies] = out_s[me]

    advance(slot + 1)
    first_copy.wait()

    def normed_load(i):
        source = (first_ref if i % 2 == 0 else first_other).at[i // 2]
        return pltpu.make_async_copy(source, normed_s.at[i % 2], normed_sem.at[i % 2])

    normed_load(0).start()
    for i in range(members):
        if i + 1 < members:
            normed_load(i + 1).start()
        rows_of = out_s[me ^ i]
        rows_of = jnp.concatenate([rows_of[t] for t in range(3)], -1)
        normed_load(i).wait()
        term = dot_tn(rows_of, normed_s[i % 2])
        heads_s[...] = term if i == 0 else heads_s[...] + term
    whole = heads_s[...].T.astype(BF16).reshape(heads_in.shape)
    heads_in[...] = jnp.where(lax.rem(me, copies) == 0, whole, jnp.zeros_like(whole))
    heads_far = remote(heads_in.at[1 - half], heads_got, far_send, far_recv, far)
    heads_far.start()
    result_copy.start()

    advance(slot + 2)
    for i in range(1, pairs):
        place = lax.rem(me // copies + i, pairs)
        pltpu.make_async_copy(
            joined_in.at[place, pl.ds(1, 2)], joined_in.at[place, pl.ds(1, 2)], out_recv.at[place]
        ).wait()
        pltpu.make_async_copy(joined_in.at[place, 0], joined_in.at[place, 0], query_recv.at[place]).wait()
    grad_first = None
    for t in range(3):
        for pair in range(pairs):
            joined_s[:, pair * LANES : (pair + 1) * LANES] = joined_in[pair, t]
        joined = joined_s[...]
        weight_load(t).wait()
        term = dot_nt(joined, weight_s[t % 2])
        grad_first = term if grad_first is None else grad_first + term
        if t == 0:
            weight_load(2).start()
        if t != 1:
            row = 4 + t // 2
            vectors_s[row : row + 1] = jnp.sum(joined.astype(F32), 0, keepdims=True)
    advance(slot + 3)
    unit, inverse = normalised(start_ref[...])
    at_input, grad_gain, grad_shift = norm_backward(grad_first, gain_ref[...], unit, inverse)
    grad_start = at_input + grad_middle_ref[...]
    run = tokens_s.shape[1]
    split = grad_start.reshape(2, run, width)
    tokens_s[...] = split.astype(BF16)
    tokens_copy = remote(tokens_s.at[1 - half], other_tokens_ref, swap_send.at[1], swap_recv.at[1], far)
    tokens_copy.start()
    own_tokens_ref[...] = jnp.where(half == 0, split[0], split[1])
    vectors_s[0:1] = jnp.sum(lead_ref[...] * grad_start, 0, keepdims=True)
    vectors_s[1:2] = jnp.sum(grad_start, 0, keepdims=True)
    vectors_s[2:3] = grad_gain
    vectors_s[3:4] = grad_shift
    vectors_s[6:10] = feed_ref[0:4]
    for i in range(up_vector_ref.shape[1] // width):
        vectors_s[10 + i : 11 + i] = up_vector_ref[:, i * width : (i + 1) * width]
    for i in range(10 + up_vector_ref.shape[1] // width, vectors_s.shape[0]):
        vectors_s[i : i + 1] = jnp.zeros((1, width), F32)
    vectors.send()

    def heads_copy(i, other):
        return remote(
            heads_got.at[other], heads_sum.at[me // copies], heads_send.at[i], heads_recv.at[me // copies],
            (base + other, grp),
        )

    def heads_begin():
        heads_far.wait_recv()
        heads_got[...] = heads_got[...] + heads_in[half]

        @pl.when(lax.rem(me, copies) == 0)
        def _():
            for i, other in enumerate(others):
                heads_copy(i, other).start()
            heads_sum[me // copies] = heads_got[me]

    def heads_middle():
        for place in range(pairs):

            @pl.when(place * copies != me)
            def _():
                pltpu.make_async_copy(heads_sum.at[place], heads_sum.at[place], heads_recv.at[place]).wait()

        heads_flow.send()

    def heads_end():
        while heads_flow.at < len(heads_flow.stages):
            heads_flow.step()
        for pair in range(pairs):
            for t in range(3):
                column = t * width + pair * LANES
                heads_ref[:, column : column + LANES] = heads_flow.held[pair, :, t * LANES : (t + 1) * LANES]

    extra = [heads_begin, vectors.step, heads_middle, vectors.step, heads_end] + [vectors.step] * len(vector_stages)
    for n, k in enumerate(slots[slot + 4]):
        if flows[k].advance():
            for copy in gather_copies(k):
                copy.start()
        if n % 2 == 1 and extra:
            extra.pop(0)()
    while extra:
        extra.pop(0)()
    vectors_ref[...] = vectors.held[...]

    for copy in grad_copies:
        copy.wait_send()
    for other in others:

        @pl.when(sends_to(other))
        def _():
            out_copy(other).wait_send()
            query_copy(other).wait_send()

    @pl.when(lax.rem(me, copies) == 0)
    def _():
        for i, other in enumerate(others):
            heads_copy(i, other).wait_send()

    for flow in flows + [vectors, heads_flow]:
        flow.drain()
    heads_far.wait_send()
    result_copy.wait()
    tokens_copy.wait()
    for k in range(count):
        for copy in gather_copies(k):
            copy.wait()


def backward(
    grad_blocks, qkv, key_aux, query, out_full, first, weight, start, grad_middle, gain, lead_rows,
    feed_vectors, up_vector, result, away, stay, plans, pairs, bands, grps, collective_id,
):
    members, _, block, _ = qkv.shape
    rows = members * block
    total, width = start.shape
    run = total // 2
    held = width // bands
    inner = up_vector.shape[1]
    arrays, count, grp_count = len(away), len(plans), bits(grps)
    shapes = [Flow.shapes(plan) for plan in plans]
    z_low = bits(bands) - 2
    links = {("band", z_low): "z", ("band", z_low + 1): "Z"}
    link = lambda stage: links.get(stage, "y" if stage[0] == "grp" else "x")
    size = lambda shape: 2 * functools.reduce(lambda m, n: m * n, shape, 1) / 2**20
    longer = rows / 2048
    tasks = [8.0] + [3.4 * longer] * members + [2.0, 4.0 * longer, 5.0, 4.0]
    slots = plan_events(
        [(size(found[0]), [link(stage) for stage in plan["stages"]]) for found, plan in zip(shapes, plans)], tasks
    )
    vector_stages = [("band", b) for b in range(bits(bands))] + [("grp", b) for b in range(grp_count)]
    longest = max(len(plan["stages"]) for plan in plans)
    vmem = pl.BlockSpec(memory_space=pltpu.VMEM)
    anywhere = pl.BlockSpec(memory_space=pl.ANY)
    dma = pltpu.SemaphoreType.DMA
    return pl.pallas_call(
        functools.partial(backward_kernel, block, members, pairs, grps, plans, slots, vector_stages),
        out_shape=(
            jax.ShapeDtypeStruct((held, inner), BF16),
            jax.ShapeDtypeStruct((inner // bands, width), BF16),
            jax.ShapeDtypeStruct((held, width), BF16),
            jax.ShapeDtypeStruct((held, 3 * width), BF16),
            jax.ShapeDtypeStruct((16, width), F32),
            jax.ShapeDtypeStruct((run, width), F32),
            jax.ShapeDtypeStruct((run, width), BF16),
            jax.ShapeDtypeStruct((run, width), BF16),
            jax.ShapeDtypeStruct(first.shape, BF16),
        ),
        in_specs=[anywhere] + [vmem] * 4 + [anywhere] * 2 + [vmem] * 6 + [anywhere] * (1 + 2 * arrays),
        out_specs=(anywhere, anywhere, anywhere, vmem, vmem, vmem, anywhere, anywhere, anywhere),
        scratch_shapes=[
            pltpu.VMEM((members, 1, block, LANES), BF16),
            pltpu.VMEM((2, rows, LANES), BF16),
            pltpu.VMEM((rows, LANES), BF16),
            pltpu.VMEM((rows, LANES), BF16),
            pltpu.VMEM((LANES, rows), F32),
            pltpu.VMEM((members, 3, block, LANES), BF16),
            pltpu.VMEM((pairs, 3, block, LANES), BF16),
            pltpu.VMEM((2, block, width), BF16),
            pltpu.VMEM((3 * LANES, width), F32),
            pltpu.VMEM((2, members, held, 3 * LANES), BF16),
            pltpu.VMEM((members, held, 3 * LANES), BF16),
            pltpu.VMEM((pairs, held, 3 * LANES), BF16),
            pltpu.VMEM((2, width, width), BF16),
            pltpu.VMEM((total, width), BF16),
            pltpu.VMEM((2, run, width), BF16),
            pltpu.VMEM((16, width), F32),
        ]
        + [pltpu.VMEM(found[0], BF16) for found in shapes]
        + [pltpu.VMEM(found[1], BF16) for found in shapes]
        + [pltpu.VMEM(shape, BF16) for found in shapes for shape in found[1:]]
        + [pltpu.VMEM((16, width), F32) for _ in vector_stages]
        + [pltpu.VMEM((pairs, held, 3 * LANES), BF16) for _ in range(grp_count)]
        + [
            dma, dma((members,)), dma((members,)), dma((members,)), dma((members,)), dma((members,)), dma((members,)),
            dma, dma, dma((2,)), dma((2,)), dma((2,)), dma((2,)),
            dma((len(vector_stages),)), dma((len(vector_stages),)), dma, dma,
            dma((members,)), dma((pairs,)), dma((grp_count,)), dma((grp_count,)),
            dma((count, grps)), dma((count, grps)), dma((count,)),
        ]
        + [dma((count,)), dma((count,)), dma((count,)), dma((count, longest)), dma((count, longest))],
        compiler_params=pltpu.CompilerParams(
            vmem_limit_bytes=60 * 2**20, collective_id=collective_id, has_side_effects=True
        ),
        cost_estimate=pl.CostEstimate(
            flops=24 * rows * rows * LANES, bytes_accessed=64 * 2**20, transcendentals=2 * rows * rows
        ),
        name="backward",
    )(
        grad_blocks, qkv, key_aux, query, out_full, first, weight, start, grad_middle, gain.reshape(1, width),
        lead_rows, feed_vectors, up_vector, result.reshape(2, run, width), *away, *stay,
    )


def swap(array, stage):
    axis, bit = stage
    size = lax.axis_size(axis)
    return lax.ppermute(array, axis, [(i, i ^ (1 << bit)) for i in range(size)])


def bit_of(stage):
    axis, bit = stage
    return (lax.axis_index(axis) >> bit) & 1


def take(array, axis, index):
    return lax.dynamic_index_in_dim(array, index, axis, keepdims=False)


def after(value, *others):
    return lax.optimization_barrier((value,) + others)[0]


def bits(size):
    return size.bit_length() - 1


def local(
    tokens,
    lead_index,
    segment,
    valid,
    lead_weight,
    lead_bias,
    first_gain,
    first_shift,
    heads_weight,
    query_bias,
    value_bias,
    output_weight,
    output_bias,
    second_gain,
    second_shift,
    up_weight,
    up_bias,
    down_weight,
    down_bias,
    cotangent,
):
    bands, grps = lax.axis_size("band"), lax.axis_size("grp")
    groups, rows, width = tokens.shape
    total = groups * rows
    pairs = width // LANES
    members = bands // groups
    band = lax.axis_index("band")
    far = ("band", bits(bands) - 1)
    own_group = bit_of(far)
    block = total

    def regroup(array):
        mine, theirs = take(array, 0, own_group), swap(take(array, 0, 1 - own_group), far)
        low = jnp.where(own_group == 0, mine, theirs)
        high = jnp.where(own_group == 0, theirs, mine)
        return jnp.concatenate([low, high], 0)

    def by_member(array):
        return take(array, 0, own_group).reshape(groups, members, rows).transpose(1, 0, 2)

    own_tokens = regroup(tokens)
    seg_rows, valid_rows = by_member(segment), by_member(valid)
    local_seg = take(seg_rows, 0, lax.rem(band, members)).reshape(total, 1)
    lead_days = take(lead_index, 0, own_group).astype(F32) * 0.25
    lead_rows = jnp.where(local_seg == 0, lead_days[0], lead_days[1])
    seg_own, valid_own = seg_rows.reshape(-1), valid_rows.reshape(-1)
    spare = jnp.arange(LANES, dtype=jnp.int32)[None, :] % HEAD_DIM
    query_aux = (spare == seg_own[:, None]).astype(BF16)
    allowed = (spare == seg_own[:, None]) & (valid_own[:, None] == 1)
    key_aux = jnp.where(
        spare < 2, jnp.where(allowed, 0.0, MASKED), jnp.where(spare < 5, 1.0, 0.0)
    ).astype(BF16)
    core = lax.rem(band, 2).astype(jnp.int32).reshape(1)
    head_bias = jnp.stack([query_bias, jnp.zeros_like(query_bias), value_bias]).reshape(3, 1, width)

    late_tokens = after(own_tokens, query_aux, key_aux, head_bias, lead_rows)
    grad_out = regroup(after(cotangent, own_tokens))
    start, first_low, blocks = heads_forward(
        late_tokens, lead_rows, lead_weight, lead_bias, first_gain, first_shift, heads_weight, head_bias
    )
    qkv, attended, out_full, query_marked = attention_forward(blocks, query_aux, key_aux, members, 1)
    attended = after(attended, grad_out)

    def normed_of(offset):
        return lax.ppermute(
            after(first_low, attended), "band", [(i, i ^ offset) for i in range(bands)]
        )

    first_rows = jnp.stack([first_low] + [normed_of(2 * k) for k in range(1, members // 2)])

    (
        result, grad_middle, grad_blocks, down_away, down_stay, up_away, up_stay,
        output_away, output_stay, feed_vectors, grad_up_bias,
    ) = feed(
        core, attended, start, grad_out, output_weight, output_bias, second_gain, second_shift,
        up_weight, up_bias, down_weight, down_bias, bands,
    )
    split = lambda v: v.reshape((2,) * (bits(bands) - 1) + v.shape[1:])
    held_up, held_down, inner = up_stay.shape[1], down_stay.shape[1], up_weight.shape[1]
    lead = [b for b in range(1, bits(bands))][::-1]
    along = {
        "x": [("band", b) for b in range(1, bits(bands) - 2)],
        "y": [("grp", b) for b in range(bits(grps))],
        "z": [("band", bits(bands) - 2)],
        "Z": [("band", bits(bands) - 1)],
    }

    def plan(array, rows_of, columns_of, links):
        stages = [stage for link in links for stage in along[link]]
        return {"array": array, "rows": rows_of, "columns": columns_of, "lead": lead, "stages": stages}

    quarter, fourth = inner // 4, held_down // 4
    up_part = lambda i, links: plan(0, (0, held_up), (i * quarter, quarter), links)
    down_part = lambda i, links: plan(1, (i * fourth, fourth), (0, width), links)
    plans = [
        up_part(0, "yzZx"),
        up_part(1, "xyzZ"),
        up_part(2, "zxyZ"),
        up_part(3, "xyzZ"),
        down_part(0, "xyzZ"),
        down_part(1, "yzZx"),
        down_part(2, "zxyZ"),
        down_part(3, "xyzZ"),
        plan(2, (0, held_up), (0, width), "yzZx"),
    ]
    grad_up, grad_down, grad_output, grad_heads, vectors, own_grads, other_grads, other_result, _ = backward(
        grad_blocks, qkv, key_aux, query_marked, out_full, first_rows, heads_weight, start, grad_middle,
        first_gain, lead_rows, feed_vectors, grad_up_bias, result,
        [split(v) for v in (up_away, down_away, output_away)],
        [split(v) for v in (up_stay, down_stay, output_stay)],
        plans, pairs, bands, grps, 3,
    )
    own_result = take(result.reshape(2, rows, width), 0, own_group)

    def assemble(mine, theirs):
        theirs = theirs.astype(mine.dtype)
        low, high = jnp.where(own_group == 0, mine, theirs), jnp.where(own_group == 0, theirs, mine)
        return jnp.stack([low, high])

    small = take(vectors[:10].reshape(10, bands, width // bands), 1, band)
    grad_up_bias = take(vectors[10 : 10 + up_weight.shape[1] // width].reshape(bands, -1), 0, band)
    wide = lambda v: v.astype(F32)
    return (
        assemble(own_result, other_result),
        assemble(own_grads, other_grads),
        small[0],
        small[1],
        small[2],
        small[3],
        wide(grad_heads),
        small[4],
        small[5],
        wide(grad_output),
        small[6],
        small[7],
        small[8],
        wide(grad_up),
        grad_up_bias,
        wide(grad_down),
        small[9],
    )


def solution(mesh):
    rows = P("grp", "band", None)
    in_specs = (rows, P("grp", None), P("grp", None), P("grp", None)) + (P(),) * 15 + (rows,)
    vector, matrix = P("band"), P("band", None)
    out_specs = (
        rows,
        rows,
        vector,
        vector,
        vector,
        vector,
        matrix,
        vector,
        vector,
        matrix,
        vector,
        vector,
        vector,
        matrix,
        vector,
        matrix,
        vector,
    )
    return jax.shard_map(local, mesh=mesh, in_specs=in_specs, out_specs=out_specs, check_vma=False)
```

```python
import functools

import jax
import jax.numpy as jnp
from jax import lax
from jax.experimental import pallas as pl
from jax.experimental.pallas import tpu as pltpu
from jax.sharding import PartitionSpec as P

HEADS = 16
HEAD_DIM = 64
LANES = 128
MESH = pl.DeviceIdType.MESH
F32 = jnp.float32
BF16 = jnp.bfloat16
VMEM_BYTES = 56 * 2**20
MASKED = -1e30


def layer_norm(values, gain, shift):
    center = values - jnp.mean(values, -1, keepdims=True)
    spread = jnp.mean(center * center, -1, keepdims=True)
    return center * lax.rsqrt(spread + 1e-05) * gain + shift


def gelu_exact(values):
    return jax.nn.gelu(values, approximate=False)


def lane_of(shape):
    return lax.broadcasted_iota(jnp.int32, shape, 1)


def in_head(shape, head):
    return lane_of(shape) // HEAD_DIM == head


def spare_lane(shape, head):
    lane = lane_of(shape)
    return jnp.where(lane // HEAD_DIM == head, LANES, lane % HEAD_DIM)


def split_terms(column, spare):
    high = column.astype(BF16).astype(F32)
    middle = (column - high).astype(BF16).astype(F32)
    low = column - high - middle
    return (
        jnp.where(spare == 2, high, 0.0)
        + jnp.where(spare == 3, middle, 0.0)
        + jnp.where(spare == 4, low, 0.0)
    )


def dot_nt(left, right):
    return lax.dot_general(left, right, (((1,), (1,)), ((), ())), preferred_element_type=F32)


def dot_tn(left, right):
    return lax.dot_general(left, right, (((0,), (0,)), ((), ())), preferred_element_type=F32)


def dot_nn(left, right):
    return jnp.dot(left, right, preferred_element_type=F32)


def forward_kernel(
    block, members, pairs,
    tokens_ref, cotangent_ref, lead_ref, segment_ref, valid_ref, lead_weight_ref, lead_bias_ref, gain_ref, shift_ref,
    weight_ref, query_bias_ref, value_bias_ref,
    qkv_ref, attended_ref, grads_ref, start_ref, first_ref, lead_out_ref, key_aux_ref, out_full_ref, query_ref,
    tokens_s, weight_s, blocks_s, query_aux, segment_s, qkv_in, key_s, value_s, out_s,
    token_sem, swap_send, swap_recv, weight_sem, local_sem, keep_sem, qkv_send, qkv_recv, out_send, out_recv,
):
    rows = members * block
    run = block // 2
    width = start_ref.shape[1]
    scale = HEAD_DIM ** (-0.5)
    copies = members // pairs
    band, grp = lax.axis_index("band"), lax.axis_index("grp")
    me = lax.rem(band, members)
    base = band - me
    others = [lax.rem(me + i, members) for i in range(1, members)]
    half, far = flip("band", bits(members))

    barrier = pltpu.get_barrier_semaphore()
    greeted = [(base + other, grp) for other in others] + [far]
    for device in greeted:
        pl.semaphore_signal(barrier, inc=1, device_id=device, device_id_type=MESH)
    pl.semaphore_wait(barrier, len(greeted))

    def remote(source, target, send, recv, device):
        return pltpu.make_async_remote_copy(
            src_ref=source, dst_ref=target, send_sem=send, recv_sem=recv, device_id=device, device_id_type=MESH
        )

    tokens_swap = remote(tokens_ref.at[1 - half], tokens_s.at[1], swap_send.at[0], swap_recv.at[0], far)
    tokens_swap.start()
    own_tokens = pltpu.make_async_copy(tokens_ref.at[half], tokens_s.at[0], token_sem)
    own_tokens.start()
    own_run = pl.ds(pl.multiple_of(half * run, run), run)
    other_run = pl.ds(pl.multiple_of((1 - half) * run, run), run)

    def weight_load(t):
        return pltpu.make_async_copy(weight_ref.at[:, pl.ds(t * width, width)], weight_s.at[t], weight_sem.at[t])

    for t in (1, 2, 0):
        weight_load(t).start()

    def in_order(ref):
        value = jnp.where(half == 0, ref[0:1], ref[1:2])
        pieces = [
            value[:, (j + r * members) * run : (j + r * members + 1) * run] for j in range(members) for r in range(2)
        ]
        return jnp.concatenate(pieces, -1)

    segment, valid = in_order(segment_ref), in_order(valid_ref)
    segment_s[...] = segment
    place = lax.broadcasted_iota(jnp.int32, (8, rows), 0)
    hidden = lambda sample: jnp.where((segment == sample) & (valid == 1), 0.0, MASKED)
    feature = jnp.where(place == 0, hidden(0), jnp.where(place == 1, hidden(1), 0.0))
    feature = jnp.where(place == 2, 1.0, feature)
    feature = jnp.where(place == 3, (segment == 0).astype(F32), feature)
    feature = jnp.where(place == 4, (segment == 1).astype(F32), feature).astype(BF16)
    row = lax.broadcasted_iota(jnp.int32, (8, LANES), 0)
    spare = lax.broadcasted_iota(jnp.int32, (8, LANES), 1) % HEAD_DIM
    for_key = ((row < 2) & (spare == row)) | ((row == 2) & (spare >= 2) & (spare <= 4))
    for_query = (row >= 3) & (row <= 4) & (spare == row - 3)
    key_aux_ref[...] = dot_tn(feature, for_key.astype(BF16)).astype(BF16)
    query_aux[...] = dot_tn(feature, for_query.astype(BF16)).astype(BF16)
    days = lead_ref[...].astype(F32) * 0.25
    days = jnp.where(half == 0, days[0:1], days[1:2])
    own_segment = segment_s[:, pl.ds(pl.multiple_of(me * block, block), block)]
    lead = jnp.where(own_segment == 0, days[:, 0:1], days[:, 1:2])
    lead = jnp.where(lax.broadcasted_iota(jnp.int32, (8, block), 0) == 0, lead, 0.0).astype(BF16)
    lead_out_ref[...] = dot_tn(lead, (row == 0).astype(BF16))

    def qkv_copy(t, phase, i, other):
        here = own_run if phase == 0 else other_run
        return remote(
            blocks_s.at[other // copies, t, here],
            qkv_in.at[me, t, here],
            qkv_send.at[t, phase, i],
            qkv_recv.at[t, phase, i],
            (base + other, grp),
        )

    def project(phase):
        here = own_run if phase == 0 else other_run
        lead_here = jnp.concatenate([lead_out_ref[here]] * (width // LANES), -1)
        start = tokens_s[phase].astype(F32) + lead_here * lead_weight_ref[...] + lead_bias_ref[...]
        start_ref[here] = start
        first = (normalised(start)[0] * gain_ref[...] + shift_ref[...]).astype(BF16)
        first_ref[here] = first
        for t in (1, 2, 0):
            if phase == 0:
                weight_load(t).wait()
            joined = dot_nn(first, weight_s[t])
            if t != 1:
                joined = joined + (query_bias_ref if t == 0 else value_bias_ref)[...]
            joined = joined.astype(BF16)
            for pair in range(pairs):
                blocks_s[pair, t, here] = joined[:, pair * LANES : (pair + 1) * LANES]
            for i, other in enumerate(others):
                qkv_copy(t, phase, i, other).start()
            qkv_in[me, t, here] = blocks_s[me // copies, t, here]

    own_tokens.wait()
    project(0)
    tokens_swap.wait_recv()
    grads_swap = remote(cotangent_ref.at[1 - half], grads_ref.at[own_run], swap_send.at[1], swap_recv.at[1], far)
    grads_own = pltpu.make_async_copy(cotangent_ref.at[half], grads_ref.at[own_run], local_sem)
    project(1)
    grads_own.start()

    for i, other in enumerate(others):
        for phase in range(2):
            qkv_copy(1, phase, i, other).wait_recv()
    keys = qkv_in[:, 1].reshape(rows, LANES)
    for head in range(2):
        key_s[head] = jnp.where(in_head(keys.shape, head), keys, key_aux_ref[...])
    for i, other in enumerate(others):
        for phase in range(2):
            qkv_copy(2, phase, i, other).wait_recv()
    value_s[...] = qkv_in[:, 2].reshape(rows, LANES)

    def sends_to(other):
        return (lax.rem(other, copies) == lax.rem(me, copies)) & (other != me)

    def out_copy(other):
        return remote(
            out_s.at[other],
            attended_ref.at[me // copies],
            out_send.at[other // copies],
            out_recv.at[me // copies],
            (base + other, grp),
        )

    @pl.loop(0, members)
    def _(i):
        other = lax.rem(me + members - i, members)

        @pl.when(i > 0)
        def _():
            for phase, here in enumerate((own_run, other_run)):
                landed = qkv_in.at[other, 0, here]
                pltpu.make_async_copy(landed, landed, qkv_recv.at[0, phase, i - 1]).wait()

        here = pl.ds(pl.multiple_of(other * block, block), block)
        query = qkv_in[other, 0].astype(F32) * scale
        aux = query_aux[here].astype(F32)
        shape = query.shape
        mixed = []
        for head in range(2):
            inside = in_head(shape, head)
            marked = jnp.where(inside, query, aux)
            scores = dot_nt(marked.astype(BF16), key_s[head])
            peak = jnp.max(scores, -1, keepdims=True)
            weights = jnp.exp(scores - peak)
            total = jnp.sum(weights, -1, keepdims=True)
            mixed.append(dot_nn(weights.astype(BF16), value_s[...]) / total)
            logsum = peak + jnp.log(total)
            marked = marked + split_terms(-logsum, spare_lane(shape, head))
            query_ref[head, here] = marked.astype(BF16)
        both = jnp.where(in_head(shape, 0), mixed[0], mixed[1])
        out_full_ref[here] = both
        out_s[other, 0] = both.astype(BF16)

        @pl.when(sends_to(other))
        def _():
            out_copy(other).start()

        @pl.when(i == 0)
        def _():
            grads_swap.start()

    keep = pltpu.make_async_copy(qkv_in, qkv_ref, keep_sem)
    keep.start()
    own_out = pltpu.make_async_copy(out_s.at[me], attended_ref.at[me // copies], token_sem)
    own_out.start()
    keep.wait()
    own_out.wait()
    grads_own.wait()
    tokens_swap.wait_send()
    for t in range(3):
        for phase in range(2):
            for i, other in enumerate(others):
                qkv_copy(t, phase, i, other).wait_send()
    for other in others:

        @pl.when(sends_to(other))
        def _():
            out_copy(other).wait_send()

    for i in range(1, pairs):
        slot = lax.rem(me // copies + i, pairs)
        pltpu.make_async_copy(attended_ref.at[slot], attended_ref.at[slot], out_recv.at[slot]).wait()
    grads_swap.wait_send()
    pltpu.make_async_copy(grads_ref.at[other_run], grads_ref.at[other_run], swap_recv.at[1]).wait()


def forward(
    tokens, cotangent, lead_index, segment, valid, lead_weight, lead_bias, gain, shift, weight, query_bias,
    value_bias, members, collective_id,
):
    _, run, width = tokens.shape
    block = 2 * run
    rows = members * block
    pairs = width // LANES
    row = lambda v: v.reshape(1, width)
    vmem = pl.BlockSpec(memory_space=pltpu.VMEM)
    anywhere = pl.BlockSpec(memory_space=pl.ANY)
    dma = pltpu.SemaphoreType.DMA
    return pl.pallas_call(
        functools.partial(forward_kernel, block, members, pairs),
        out_shape=(
            jax.ShapeDtypeStruct((members, 3, block, LANES), BF16),
            jax.ShapeDtypeStruct((pairs, 1, block, LANES), BF16),
            jax.ShapeDtypeStruct((block, width), BF16),
            jax.ShapeDtypeStruct((block, width), F32),
            jax.ShapeDtypeStruct((block, width), BF16),
            jax.ShapeDtypeStruct((block, LANES), F32),
            jax.ShapeDtypeStruct((rows, LANES), BF16),
            jax.ShapeDtypeStruct((rows, LANES), F32),
            jax.ShapeDtypeStruct((2, rows, LANES), BF16),
        ),
        in_specs=[anywhere, anywhere] + [vmem] * 7 + [anywhere, vmem, vmem],
        out_specs=(anywhere, anywhere, anywhere) + (vmem,) * 6,
        scratch_shapes=[
            pltpu.VMEM((2, run, width), BF16),
            pltpu.VMEM((3, width, width), BF16),
            pltpu.VMEM((pairs, 3, block, LANES), BF16),
            pltpu.VMEM((rows, LANES), BF16),
            pltpu.VMEM((1, rows), jnp.int32),
            pltpu.VMEM((members, 3, block, LANES), BF16),
            pltpu.VMEM((2, rows, LANES), BF16),
            pltpu.VMEM((rows, LANES), BF16),
            pltpu.VMEM((members, 1, block, LANES), BF16),
            dma, dma((2,)), dma((2,)), dma((3,)), dma, dma,
            dma((3, 2, members)), dma((3, 2, members)), dma((members,)), dma((members,)),
        ],
        compiler_params=pltpu.CompilerParams(
            vmem_limit_bytes=VMEM_BYTES, collective_id=collective_id, has_side_effects=True
        ),
        cost_estimate=pl.CostEstimate(
            flops=8 * rows * rows * LANES, bytes_accessed=32 * 2**20, transcendentals=2 * rows * rows
        ),
        name="forward",
    )(
        tokens, cotangent, lead_index, segment, valid, row(lead_weight), row(lead_bias), row(gain), row(shift),
        weight, row(query_bias), row(value_bias),
    )


def device_at(axis, index):
    band, grp = lax.axis_index("band"), lax.axis_index("grp")
    return (index, grp) if axis == "band" else (band, index)


def flip(axis, bit):
    index = lax.axis_index(axis)
    mine = lax.rem(index // (1 << bit), 2)
    return mine, device_at(axis, index + (1 - 2 * mine) * (1 << bit))


def normalised(values):
    center = values - jnp.mean(values, -1, keepdims=True)
    spread = jnp.mean(center * center, -1, keepdims=True)
    inverse = lax.rsqrt(spread + 1e-05)
    return center * inverse, inverse


def norm_backward(grads, gain, unit, inverse):
    inner = grads * gain
    at_input = inverse * (
        inner
        - jnp.mean(inner, -1, keepdims=True)
        - unit * jnp.mean(inner * unit, -1, keepdims=True)
    )
    return at_input, jnp.sum(grads * unit, 0, keepdims=True), jnp.sum(grads, 0, keepdims=True)


def by_core(value, core, held, away_ref, stay_ref):
    split = value.astype(BF16).reshape(-1, 2, held, value.shape[-1])
    even, odd = split[:, 0], split[:, 1]
    away_ref[...] = jnp.where(core == 0, odd, even)
    stay_ref[...] = jnp.where(core == 0, even, odd)


def constant(*shape):
    return pl.BlockSpec(shape, lambda *i: (0,) * len(shape))


def feed_kernel(
    core_ref, attended_ref, start_ref, grad_ref, output_weight_ref, output_bias_ref, gain_ref, shift_ref,
    up_ref, up_bias_ref, down_ref, down_bias_ref,
    result_ref, grad_middle_ref, grad_attended_ref, down_away, down_stay, up_away, up_stay,
    output_away, output_stay, vectors_ref, up_vector_ref,
    attended_s, middle_s, unit_s, inverse_s, second_s, second_turned, result_s, grad_second_s,
):
    step, steps = pl.program_id(0), pl.num_programs(0)
    core = core_ref[0]
    pairs = attended_ref.shape[0]

    @pl.when(step == 0)
    def _():
        for pair in range(pairs):
            attended_s[:, pair * LANES : (pair + 1) * LANES] = attended_ref[pair, 0]
        middle = (
            start_ref[...] + dot_nn(attended_s[...], output_weight_ref[...]) + output_bias_ref[...]
        )
        middle_s[...] = middle
        unit, inverse = normalised(middle)
        unit_s[...] = unit
        inverse_s[...] = inverse
        second = unit * gain_ref[...] + shift_ref[...]
        second_s[...] = second.astype(BF16)
        second_turned[...] = second.T.astype(BF16)
        result_s[...] = jnp.zeros_like(result_s)
        grad_second_s[...] = jnp.zeros_like(grad_second_s)

    grads = grad_ref[...]
    upper = dot_nn(second_s[...], up_ref[...]) + up_bias_ref[...]
    level = 0.5 + 0.5 * lax.erf(upper * 0.7071067811865476)
    hidden = (upper * level).astype(BF16)
    slope = level + upper * (0.3989422804014327 * jnp.exp(-0.5 * upper * upper))
    result_s[...] += dot_nn(hidden, down_ref[...])
    by_core(dot_tn(hidden, grads), core, down_away.shape[1], down_away, down_stay)
    grad_upper_wide = dot_nt(grads, down_ref[...]) * slope
    grad_upper = grad_upper_wide.astype(BF16)
    up_vector_ref[...] = jnp.sum(grad_upper.astype(F32), 0, keepdims=True)
    by_core(dot_nn(second_turned[...], grad_upper), core, up_away.shape[1], up_away, up_stay)
    grad_second_s[...] += dot_nt(grad_upper, up_ref[...])

    @pl.when(step == steps - 1)
    def _():
        result_ref[...] = (middle_s[...] + result_s[...] + down_bias_ref[...]).astype(BF16)
        wide = grads.astype(F32)
        at_input, grad_gain, grad_shift = norm_backward(
            grad_second_s[...], gain_ref[...], unit_s[...], inverse_s[...]
        )
        grad_middle = at_input + wide
        grad_middle_ref[...] = grad_middle
        branch = grad_middle.astype(BF16)
        by_core(dot_tn(attended_s[...], branch), core, output_away.shape[1], output_away, output_stay)
        grad_attended = dot_nt(branch, output_weight_ref[...]).astype(BF16)
        for pair in range(pairs):
            grad_attended_ref[pair, 0] = grad_attended[:, pair * LANES : (pair + 1) * LANES]
        vectors_ref[0:1] = jnp.sum(branch.astype(F32), 0, keepdims=True)
        vectors_ref[1:2] = grad_gain
        vectors_ref[2:3] = grad_shift
        vectors_ref[3:4] = jnp.sum(wide, 0, keepdims=True)


def feed(core, attended, start, grads, output_weight, output_bias, gain, shift, up, up_bias, down, down_bias, bands):
    total, width = start.shape
    inner = up.shape[1]
    pairs = width // LANES
    chunk = 1024
    held, held_down = width // bands, inner // bands
    per_chunk = chunk // held_down // 2
    row = lambda v: v.reshape(1, -1)
    half = bands // 2
    one = lambda *shape: constant(*shape)
    return pl.pallas_call(
        feed_kernel,
        grid_spec=pltpu.PrefetchScalarGridSpec(
            num_scalar_prefetch=1,
            grid=(inner // chunk,),
            in_specs=[
                one(pairs, 1, total, LANES),
                one(total, width),
                one(total, width),
                one(width, width),
                one(1, width),
                one(1, width),
                one(1, width),
                pl.BlockSpec((width, chunk), lambda j, c: (0, j)),
                pl.BlockSpec((1, chunk), lambda j, c: (0, j)),
                pl.BlockSpec((chunk, width), lambda j, c: (j, 0)),
                one(1, width),
            ],
            out_specs=(
                one(total, width),
                one(total, width),
                one(pairs, 1, total, LANES),
                pl.BlockSpec((per_chunk, held_down, width), lambda j, c: (j, 0, 0)),
                pl.BlockSpec((per_chunk, held_down, width), lambda j, c: (j, 0, 0)),
                pl.BlockSpec((half, held, chunk), lambda j, c: (0, 0, j)),
                pl.BlockSpec((half, held, chunk), lambda j, c: (0, 0, j)),
                one(half, held, width),
                one(half, held, width),
                one(8, width),
                pl.BlockSpec((1, chunk), lambda j, c: (0, j)),
            ),
            scratch_shapes=[
                pltpu.VMEM((total, width), BF16),
                pltpu.VMEM((total, width), F32),
                pltpu.VMEM((total, width), F32),
                pltpu.VMEM((total, 1), F32),
                pltpu.VMEM((total, width), BF16),
                pltpu.VMEM((width, total), BF16),
                pltpu.VMEM((total, width), F32),
                pltpu.VMEM((total, width), F32),
            ],
        ),
        out_shape=(
            jax.ShapeDtypeStruct((total, width), BF16),
            jax.ShapeDtypeStruct((total, width), F32),
            jax.ShapeDtypeStruct((pairs, 1, total, LANES), BF16),
            jax.ShapeDtypeStruct((half, held_down, width), BF16),
            jax.ShapeDtypeStruct((half, held_down, width), BF16),
            jax.ShapeDtypeStruct((half, held, inner), BF16),
            jax.ShapeDtypeStruct((half, held, inner), BF16),
            jax.ShapeDtypeStruct((half, held, width), BF16),
            jax.ShapeDtypeStruct((half, held, width), BF16),
            jax.ShapeDtypeStruct((8, width), F32),
            jax.ShapeDtypeStruct((1, inner), F32),
        ),
        compiler_params=pltpu.CompilerParams(vmem_limit_bytes=VMEM_BYTES),
        cost_estimate=pl.CostEstimate(
            flops=12 * total * width * inner, bytes_accessed=8 * width * inner, transcendentals=2 * total * inner
        ),
        name="feed",
    )(
        core, attended, start, grads, output_weight, row(output_bias), row(gain), row(shift),
        up, row(up_bias), down, row(down_bias),
    )


LINK = 26.0
CORE = 1.55
ADD = 0.4
HOP = 4.0


def plan_steps(sizes, stages, vector_stages, iterations, iteration, slack, late_slack):
    free = {link: 0.0 for link in ("x", "y", "z", "Z", "core")}
    held, left, orders = list(sizes), [list(stages) for _ in sizes], [[] for _ in sizes]
    ready, waiting, steps, count = [], [], [], 0
    now = 3.0

    def occupy(link, size):
        if link == "Z":
            free["Z"] = max(now, free["Z"]) + 2 * size * LINK
            free["z"] = max(now, free["z"]) + size * LINK
        else:
            free[link] = max(now, free[link]) + size * (CORE if link == "core" else LINK)
        return free[link] + HOP

    def expect(arrival, name, argument=None):
        nonlocal count
        count += 1
        waiting.append((arrival, count, name, argument))

    def send_ready(limit):
        sent = True
        while sent:
            sent = False
            for link in sorted("xyzZ", key=lambda l: free[l]):
                fit = [
                    k
                    for k in ready
                    if any(stages[s] == link for s in left[k])
                    and (link != "Z" or len(orders[k]) >= len(stages) - 1)
                ]
                if free[link] - now >= limit or not fit:
                    continue
                k = max(fit, key=lambda k: len(left[k]))
                stage = [s for s in left[k] if stages[s] == link][0]
                left[k].remove(stage)
                orders[k].append(stage)
                held[k] /= 2
                ready.remove(k)
                steps.append(("send", k))
                expect(occupy(link, held[k]), "take", k)
                sent = True
                break

    def vector_hop(name, hop):
        if hop < len(vector_stages):
            expect(occupy(stages.get(vector_stages[hop], "core"), 0.035), name, hop)

    def perform(name, argument):
        nonlocal now
        steps.append((name, argument))
        if name == "take":
            k = argument
            now += held[k] * ADD + 0.1
            if left[k]:
                ready.append(k)
            else:
                occupy("y", held[k])
        elif name in ("early", "late"):
            now += 0.2
            vector_hop(name, argument + 1)
        elif name == "grads":
            now += 3.0
            expect(now, "iteration", 0)
        elif name == "iteration":
            now += iteration
            for link in "xz":
                occupy(link, 0.5 / iterations)
            if argument + 1 < iterations:
                expect(now, "iteration", argument + 1)
            else:
                expect(now, "queries")
        elif name == "queries":
            now += 2.0
            expect(max(occupy("x", 0.25), occupy("z", 0.25)), "joined")
            expect(now, "products")
        elif name == "products":
            now += 4.5
            expect(occupy("y", 0.19), "near")
        elif name == "joined":
            now += 5.0
            expect(now, "start")
        elif name == "start":
            now += 3.0
            occupy("Z", 0.25)
            vector_hop("late", 0)
        elif name == "near":
            now += 0.3
            expect(occupy("Z", 0.1), "far")
        elif name == "far":
            now += 0.3
            expect(max(occupy("x", 0.06), occupy("z", 0.06)), "members")
        elif name == "members":
            now += 0.3
            expect(occupy("y", 0.1), "rows")
        elif name == "rows":
            now += 0.5

    expect(max(occupy("x", 0.25), occupy("z", 0.25)), "grads")
    for k, size in enumerate(sizes):
        expect(occupy("core", size), "take", k)
    occupy("Z", 0.25)
    vector_hop("early", 0)
    main = ("grads", "iteration", "queries", "products", "joined", "start")
    while waiting or ready:
        if not waiting:
            send_ready(1e9)
        arrived = [w for w in waiting if w[0] <= now]
        others = [w for w in arrived if w[2] not in main]
        chosen = min(others or arrived or waiting)
        waiting.remove(chosen)
        now = max(now, chosen[0])
        perform(*chosen[2:])
        looped = any(w[2] in ("grads", "iteration") for w in waiting)
        send_ready(slack if looped else late_slack)
    return orders, steps, now, free


class Flow:
    def __init__(self, k, plan, away, stay, core_in, stay_s, buffers, sems):
        self.k, self.plan, self.away, self.stay = k, plan, away, stay
        self.core_in, self.stay_s, self.buffers = core_in, stay_s, buffers
        self.core_send, self.core_recv, self.stay_sem, self.send_sem, self.recv_sem = sems
        self.stages, self.lead = plan["stages"], list(plan["lead"])
        self.flips = [flip(*stage) for stage in self.stages]
        self.core_other = flip("band", 0)[1]
        self.held, self.at = None, -1

    @staticmethod
    def shapes(plan):
        shape, lead = [2] * len(plan["lead"]) + [plan["rows"][1], plan["columns"][1]], list(plan["lead"])
        found = [tuple(shape)]
        for axis, bit in plan["stages"]:
            if axis == "band":
                at = lead.index(bit)
                del shape[at], lead[at]
            else:
                shape[-1] //= 2
            found.append(tuple(shape))
        return found

    def region(self, stage, index):
        (first, rows), (column, columns) = self.plan["rows"], self.plan["columns"]
        where = [slice(None)] * len(self.plan["lead"]) + [pl.ds(first, rows), pl.ds(column, columns)]
        if stage is not None:
            axis, bit = stage
            if axis == "band":
                where[self.plan["lead"].index(bit)] = index
            else:
                half = columns // 2
                where[-1] = pl.ds(pl.multiple_of(column + index * half, LANES), half)
        return tuple(where)

    def pick(self, ref, index):
        axis, bit = self.stages[self.at]
        where = [slice(None)] * len(ref.shape)
        if axis == "band":
            where[self.lead.index(bit)] = index
        else:
            half = ref.shape[-1] // 2
            where[-1] = pl.ds(pl.multiple_of(index * half, LANES), half)
        return tuple(where)

    def core_copy(self):
        return pltpu.make_async_remote_copy(
            src_ref=self.away.at[self.region(None, None)],
            dst_ref=self.core_in,
            send_sem=self.core_send.at[self.k],
            recv_sem=self.core_recv.at[self.k],
            device_id=self.core_other,
            device_id_type=MESH,
        )

    def stay_copy(self, index):
        return pltpu.make_async_copy(
            self.stay.at[self.region(self.stages[0], index)], self.stay_s, self.stay_sem.at[self.k]
        )

    def stage_copy(self, stage, source):
        return pltpu.make_async_remote_copy(
            src_ref=source,
            dst_ref=self.buffers[stage],
            send_sem=self.send_sem.at[self.k, stage],
            recv_sem=self.recv_sem.at[self.k, stage],
            device_id=self.flips[stage][1],
            device_id_type=MESH,
        )

    def start(self):
        self.core_copy().start()
        self.stay_copy(1 - self.flips[0][0]).start()

    def take(self):
        if self.at < 0:
            self.at = 0
            mine = self.flips[0][0]
            self.core_copy().wait_recv()
            self.stay_copy(1 - mine).wait()
            away = self.pick(self.core_in, 1 - mine)
            self.core_in[away] = self.core_in[away] + self.stay_s[...]
            self.stay_copy(mine).start()
            self.held = self.core_in
            return False
        mine = self.flips[self.at][0]
        buffer = self.buffers[self.at]
        self.stage_copy(self.at, buffer).wait_recv()
        kept = self.held[self.pick(self.held, mine)]
        if self.at == 0:
            self.stay_copy(mine).wait()
            kept = kept + self.stay_s[...]
        buffer[...] = buffer[...] + kept
        axis, bit = self.stages[self.at]
        if axis == "band":
            self.lead.remove(bit)
        self.held = buffer
        self.at += 1
        return self.at == len(self.stages)

    def send(self):
        self.stage_copy(self.at, self.held.at[self.pick(self.held, 1 - self.flips[self.at][0])]).start()

    def drain(self):
        self.core_copy().wait_send()
        for stage, buffer in enumerate(self.buffers):
            self.stage_copy(stage, buffer).wait_send()


class FullFlow:
    def __init__(self, held, stages, buffers, send_sem, recv_sem):
        self.held, self.stages, self.buffers = held, stages, buffers
        self.send_sem, self.recv_sem = send_sem, recv_sem
        self.flips = [flip(*stage) for stage in stages]
        self.at = 0

    def copy(self, stage, source):
        return pltpu.make_async_remote_copy(
            src_ref=source,
            dst_ref=self.buffers[stage],
            send_sem=self.send_sem.at[stage],
            recv_sem=self.recv_sem.at[stage],
            device_id=self.flips[stage][1],
            device_id_type=MESH,
        )

    def send(self):
        if self.at < len(self.stages):
            self.copy(self.at, self.held).start()

    def step(self):
        if self.at < len(self.stages):
            buffer = self.buffers[self.at]
            self.copy(self.at, buffer).wait_recv()
            buffer[...] = buffer[...] + self.held[...]
            self.held = buffer
            self.at += 1
            self.send()

    def drain(self):
        for stage, buffer in enumerate(self.buffers):
            self.copy(stage, buffer).wait_send()


def backward_kernel(
    block, members, pairs, grps, plans, steps, vector_stages,
    grad_ref, qkv_ref, key_aux_ref, query_ref, out_full_ref, weight_ref, start_ref, grad_middle_ref, gain_ref, lead_ref, feed_ref, up_vector_ref, result_ref, *refs,
):
    count = len(plans)
    arrays = max(plan["array"] for plan in plans) + 1
    refs = list(refs)
    firsts = members // 2

    def grab(n):
        found = refs[:n]
        del refs[:n]
        return found

    first_refs, away_refs, stay_refs = grab(firsts), grab(arrays), grab(arrays)
    up_ref, down_ref, output_ref, heads_ref, late_ref, early_ref = grab(6)
    own_tokens_ref, other_tokens_ref, other_result_ref, first_other = grab(4)
    grad_in, grad_s, query_s, plain_s, query_sum, out_s, joined_in = grab(7)
    normed_s, heads_s, heads_in, heads_near, heads_got, heads_sum, heads_rows = grab(7)
    weight_s, joined_s, tokens_s, late_s, early_s, grad_first = grab(6)
    core_in, stay_s = grab(count), grab(count)
    buffers = [grab(len(plan["stages"])) for plan in plans]
    late_buffers, early_buffers = grab(len(vector_stages)), grab(len(vector_stages))
    grp_count = bits(grps)
    heads_buffers = grab(grp_count - 1)
    (
        local_sem, grad_send, grad_recv, out_send, out_recv, query_send, query_recv, first_send, first_recv,
        normed_sem, weight_sem, swap_send, swap_recv, late_send, late_recv, early_send, early_recv, far_send, far_recv,
        heads_send, heads_recv, heads_two_send, heads_two_recv, gather_send, gather_recv, own_sem,
        near_send, near_recv, rows_send, rows_recv,
    ) = grab(30)
    flow_sems = grab(5)

    rows = key_aux_ref.shape[0]
    width = start_ref.shape[1]
    scale = HEAD_DIM ** (-0.5)
    copies = members // pairs
    band, grp = lax.axis_index("band"), lax.axis_index("grp")
    me = lax.rem(band, members)
    base = band - me
    others = [lax.rem(me + i, members) for i in range(1, members)]
    groups_off = [lax.rem(grp + i, grps) for i in range(1, grps)]
    half, far = flip("band", bits(members))
    core_other = flip("band", 0)[1]
    flows = [
        Flow(k, plan, away_refs[plan["array"]], stay_refs[plan["array"]], core_in[k], stay_s[k], buffers[k], flow_sems)
        for k, plan in enumerate(plans)
    ]
    late = FullFlow(late_s, vector_stages, late_buffers, late_send, late_recv)
    early = FullFlow(early_s, vector_stages, early_buffers, early_send, early_recv)
    heads_flow = FullFlow(
        heads_near, [("grp", b) for b in range(1, grp_count)], heads_buffers, heads_two_send, heads_two_recv
    )
    near_mine, near = flip("grp", 0)
    near_rows = heads_near.shape[2]
    own_rows = pl.ds(pl.multiple_of(near_mine * near_rows, near_rows), near_rows)
    sent_rows = pl.ds(pl.multiple_of((1 - near_mine) * near_rows, near_rows), near_rows)

    barrier = pltpu.get_barrier_semaphore()
    greeted = [(base + other, grp) for other in others] + [(band, g) for g in groups_off] + [far]
    for device in greeted:
        pl.semaphore_signal(barrier, inc=1, device_id=device, device_id_type=MESH)
    pl.semaphore_wait(barrier, len(greeted))

    def remote(source, target, send, recv, device):
        return pltpu.make_async_remote_copy(
            src_ref=source, dst_ref=target, send_sem=send, recv_sem=recv, device_id=device, device_id_type=MESH
        )

    grad_copies = [
        remote(
            grad_ref.at[other // copies], grad_in.at[me], grad_send.at[i], grad_recv.at[i], (base + other, grp)
        )
        for i, other in enumerate(others)
    ]
    for copy in grad_copies:
        copy.start()
    own = pltpu.make_async_copy(grad_ref.at[me // copies], grad_in.at[me], local_sem)
    own.start()
    for flow in flows:
        flow.start()
    first_copies = [
        remote(first_refs[k], first_other.at[k], first_send.at[k], first_recv.at[k], core_other) for k in range(firsts)
    ]
    for copy in first_copies:
        copy.start()
    result_copy = remote(result_ref.at[1 - half], other_result_ref, swap_send.at[0], swap_recv.at[0], far)
    result_copy.start()

    def weight_load(t):
        return pltpu.make_async_copy(
            weight_ref.at[:, pl.ds(t * width, width)], weight_s.at[t % 2], weight_sem.at[t % 2]
        )

    for t in range(2):
        weight_load(t).start()
    early_s[0:4] = feed_ref[0:4]
    for i in range(4):
        early_s[4 + i : 5 + i] = up_vector_ref[:, i * width : (i + 1) * width]
    early.send()
    query_s[...] = qkv_ref[:, 0].reshape(rows, LANES)
    query_sum[...] = jnp.zeros_like(query_sum)

    gathers = []

    def gather_copies(k):
        plan, flow = plans[k], flows[k]
        target = (up_ref, down_ref, output_ref)[plan["array"]]
        size = plan["columns"][1]
        columns = size >> grp_count
        offset = plan["columns"][0]
        for b in range(grp_count):
            size //= 2
            offset = offset + flip("grp", b)[0] * size
        where = target.at[pl.ds(*plan["rows"]), pl.ds(pl.multiple_of(offset, LANES), columns)]
        held = flow.buffers[-1]
        mine = pltpu.make_async_copy(held, where, own_sem.at[k])
        return [mine] + [
            remote(held, where, gather_send.at[k, i], gather_recv.at[k, i], (band, g))
            for i, g in enumerate(groups_off)
        ]

    slots = [[]]
    for step in steps:
        if step[0] in ("grads", "iteration", "queries"):
            slots.append([])
        else:
            slots[-1].append(step)
    rest = slots.pop()

    def small_step(name, argument):
        if name == "send":
            flows[argument].send()
        elif name == "early":
            early.step()
        elif name == "late":
            late.step()
        elif flows[argument].take():
            for copy in gather_copies(argument):
                copy.start()

    def advance(slot):
        for step in slots[slot]:
            small_step(*step)

    advance(0)
    own.wait()
    for copy in grad_copies:
        copy.wait_recv()
    grads = grad_in[...].reshape(rows, LANES)
    plain_s[...] = grads
    wide = grads.astype(F32)
    product = wide * out_full_ref[...]
    for head in range(2):
        inside = in_head(wide.shape, head)
        delta = jnp.sum(jnp.where(inside, product, 0.0), -1, keepdims=True)
        marked = jnp.where(inside, wide, split_terms(-delta, spare_lane(wide.shape, head)))
        grad_s[head] = marked.astype(BF16)

    def sends_to(other):
        return (lax.rem(other, copies) == lax.rem(me, copies)) & (other != me)

    def out_copy(other):
        return remote(
            out_s.at[other, pl.ds(1, 2)],
            joined_in.at[me // copies, pl.ds(1, 2)],
            out_send.at[other // copies],
            out_recv.at[me // copies],
            (base + other, grp),
        )

    def query_copy(other):
        return remote(
            out_s.at[other, 0],
            joined_in.at[me // copies, 0],
            query_send.at[other // copies],
            query_recv.at[me // copies],
            (base + other, grp),
        )

    sub = min(block, 2**19 // rows)

    @pl.loop(0, members)
    def _(i):
        for slot in range(1, 1 + members):
            if slots[slot]:

                @pl.when(i == slot - 1)
                def _(slot=slot):
                    advance(slot)

        other = lax.rem(me + 1 + i, members)
        for low in range(0, block, sub):
            here = pl.ds(pl.multiple_of(other * block + low, sub), sub)
            key = qkv_ref[other, 1, pl.ds(low, sub)]
            value = qkv_ref[other, 2, pl.ds(low, sub)]
            aux = key_aux_ref[here]
            shape = key.shape
            grad_key, grad_value = [], []
            for head in range(2):
                inside = in_head(shape, head)
                spare = spare_lane(shape, head)
                ones = jnp.where((spare >= 2) & (spare <= 4), 1.0, 0.0).astype(BF16)
                probs = jnp.exp(dot_nt(jnp.where(inside, key, aux), query_ref[head]))
                grad_probs = dot_nt(jnp.where(inside, value, ones), grad_s[head])
                grad_scores = (probs * grad_probs).astype(BF16)
                grad_value.append(dot_nn(probs.astype(BF16), plain_s[...]))
                grad_key.append(dot_nn(grad_scores, query_s[...]))
                query_sum[...] += dot_tn(jnp.where(inside, key, jnp.zeros_like(key)), grad_scores)
            first = in_head(shape, 0)
            out_s[other, 1, pl.ds(low, sub)] = (jnp.where(first, grad_key[0], grad_key[1]) * scale).astype(BF16)
            out_s[other, 2, pl.ds(low, sub)] = jnp.where(first, grad_value[0], grad_value[1]).astype(BF16)

        @pl.when(sends_to(other))
        def _():
            out_copy(other).start()

    advance(members + 1)
    out_s[:, 0] = (query_sum[...].T * scale).astype(BF16).reshape(members, block, LANES)
    for other in others:

        @pl.when(sends_to(other))
        def _():
            query_copy(other).start()

    joined_in[me // copies] = out_s[me]

    def normed_load(i):
        source = first_refs[i // 2] if i % 2 == 0 else first_other.at[i // 2]
        return pltpu.make_async_copy(source, normed_s.at[i % 2], normed_sem.at[i % 2])

    def near_copy():
        return remote(heads_in.at[:, :, sent_rows], heads_near, near_send, near_recv, near)

    def far_copy():
        return remote(heads_flow.held.at[1 - half], heads_got, far_send, far_recv, far)

    def tokens_copy():
        return remote(tokens_s.at[1 - half], other_tokens_ref, swap_send.at[1], swap_recv.at[1], far)

    def heads_copy(i, other):
        return remote(
            heads_got.at[other], heads_sum.at[me // copies], heads_send.at[i], heads_recv.at[me // copies],
            (base + other, grp),
        )

    def rows_copy():
        return remote(heads_sum, heads_rows.at[:, own_rows], rows_send, rows_recv, near)

    def products_step():
        for copy in first_copies:
            copy.wait_recv()
        normed_load(0).start()
        for i in range(members):
            if i + 1 < members:
                normed_load(i + 1).start()
            rows_of = out_s[me ^ i]
            rows_of = jnp.concatenate([rows_of[t] for t in range(3)], -1)
            normed_load(i).wait()
            term = dot_tn(rows_of, normed_s[i % 2])
            heads_s[...] = term if i == 0 else heads_s[...] + term
        whole = heads_s[...].T.astype(BF16).reshape(heads_in.shape)
        heads_in[...] = jnp.where(lax.rem(me, copies) == 0, whole, jnp.zeros_like(whole))
        near_copy().start()

    def joined_step():
        for i in range(1, pairs):
            place = lax.rem(me // copies + i, pairs)
            pltpu.make_async_copy(
                joined_in.at[place, pl.ds(1, 2)], joined_in.at[place, pl.ds(1, 2)], out_recv.at[place]
            ).wait()
            pltpu.make_async_copy(joined_in.at[place, 0], joined_in.at[place, 0], query_recv.at[place]).wait()
        for t in range(3):
            for pair in range(pairs):
                joined_s[:, pair * LANES : (pair + 1) * LANES] = joined_in[pair, t]
            joined = joined_s[...]
            weight_load(t).wait()
            term = dot_nt(joined, weight_s[t % 2])
            grad_first[...] = term if t == 0 else grad_first[...] + term
            if t == 0:
                weight_load(2).start()
            if t != 1:
                row = 4 + t // 2
                late_s[row : row + 1] = jnp.sum(joined.astype(F32), 0, keepdims=True)

    def start_step():
        unit, inverse = normalised(start_ref[...])
        at_input, grad_gain, grad_shift = norm_backward(grad_first[...], gain_ref[...], unit, inverse)
        grad_start = at_input + grad_middle_ref[...]
        split = grad_start.reshape((2,) + own_tokens_ref.shape)
        tokens_s[...] = split.astype(BF16)
        tokens_copy().start()
        own_tokens_ref[...] = jnp.where(half == 0, split[0], split[1])
        lead = jnp.concatenate([lead_ref[...]] * (width // LANES), -1)
        late_s[0:1] = jnp.sum(lead * grad_start, 0, keepdims=True)
        late_s[1:2] = jnp.sum(grad_start, 0, keepdims=True)
        late_s[2:3] = grad_gain
        late_s[3:4] = grad_shift
        late_s[6:8] = jnp.zeros((2, width), F32)
        late.send()

    def near_step():
        near_copy().wait_recv()
        heads_near[...] = heads_near[...] + heads_in[:, :, own_rows]
        heads_flow.send()
        while heads_flow.at < len(heads_flow.stages):
            heads_flow.step()
        far_copy().start()

    def far_step():
        far_copy().wait_recv()
        heads_got[...] = heads_got[...] + heads_flow.held[half]

        @pl.when(lax.rem(me, copies) == 0)
        def _():
            for i, other in enumerate(others):
                heads_copy(i, other).start()
            heads_sum[me // copies] = heads_got[me]

    def members_step():
        for place in range(pairs):

            @pl.when(place * copies != me)
            def _():
                pltpu.make_async_copy(heads_sum.at[place], heads_sum.at[place], heads_recv.at[place]).wait()

        rows_copy().start()
        heads_rows[:, own_rows] = heads_sum[...]

    def rows_step():
        rows_copy().wait_recv()
        for pair in range(pairs):
            for t in range(3):
                column = t * width + pair * LANES
                heads_ref[:, column : column + LANES] = heads_rows[pair, :, t * LANES : (t + 1) * LANES]

    large = {
        "products": products_step, "joined": joined_step, "start": start_step, "near": near_step,
        "far": far_step, "members": members_step, "rows": rows_step,
    }
    for name, argument in rest:
        if name in large:
            large[name]()
        else:
            small_step(name, argument)
    late_ref[...] = late.held[...]
    early_ref[...] = early.held[...]

    for copy in grad_copies:
        copy.wait_send()
    for other in others:

        @pl.when(sends_to(other))
        def _():
            out_copy(other).wait_send()
            query_copy(other).wait_send()

    @pl.when(lax.rem(me, copies) == 0)
    def _():
        for i, other in enumerate(others):
            heads_copy(i, other).wait_send()

    for flow in flows + [late, early, heads_flow]:
        flow.drain()
    near_copy().wait_send()
    rows_copy().wait_send()
    far_copy().wait_send()
    for copy in first_copies:
        copy.wait_send()
    result_copy.wait()
    tokens_copy().wait()
    for k in range(count):
        for copy in gather_copies(k):
            copy.wait()


def backward(
    grad_blocks, qkv, key_aux, query, out_full, first, weight, start, grad_middle, gain, lead_rows,
    feed_vectors, up_vector, result, away, stay, plans, pairs, bands, grps, collective_id,
):
    members, _, block, _ = qkv.shape
    rows = members * block
    total, width = start.shape
    run = total // 2
    held = width // bands
    inner = up_vector.shape[1]
    arrays, count, grp_count = len(away), len(plans), bits(grps)
    z_low = bits(bands) - 2
    links = {("band", z_low): "z", ("band", z_low + 1): "Z"}
    links.update({("band", b): "x" for b in range(1, z_low)})
    links.update({("grp", b): "y" for b in range(grp_count)})
    vector_stages = [("band", b) for b in range(bits(bands))] + [("grp", b) for b in range(grp_count)]
    sizes = [2**bits(bands) * plan["rows"][1] * plan["columns"][1] / 2**20 for plan in plans]
    orders, steps, _, _ = plan_steps(sizes, links, vector_stages, members, 4.0 * rows / 2048, 7.0, 5.0)
    plans = [dict(plan, stages=order) for plan, order in zip(plans, orders)]
    shapes = [Flow.shapes(plan) for plan in plans]
    longest = max(len(plan["stages"]) for plan in plans)
    vmem = pl.BlockSpec(memory_space=pltpu.VMEM)
    anywhere = pl.BlockSpec(memory_space=pl.ANY)
    dma = pltpu.SemaphoreType.DMA
    return pl.pallas_call(
        functools.partial(backward_kernel, block, members, pairs, grps, plans, steps, vector_stages),
        out_shape=(
            jax.ShapeDtypeStruct((held, inner), BF16),
            jax.ShapeDtypeStruct((inner // bands, width), BF16),
            jax.ShapeDtypeStruct((held, width), BF16),
            jax.ShapeDtypeStruct((held, 3 * width), BF16),
            jax.ShapeDtypeStruct((8, width), F32),
            jax.ShapeDtypeStruct((8, width), F32),
            jax.ShapeDtypeStruct((run, width), F32),
            jax.ShapeDtypeStruct((run, width), BF16),
            jax.ShapeDtypeStruct((run, width), BF16),
            jax.ShapeDtypeStruct((len(first),) + first[0].shape, BF16),
        ),
        in_specs=[anywhere] + [vmem] * 4 + [anywhere] + [vmem] * 6 + [anywhere] * (1 + len(first) + 2 * arrays),
        out_specs=(anywhere, anywhere, anywhere, vmem, vmem, vmem, vmem, anywhere, anywhere, anywhere),
        scratch_shapes=[
            pltpu.VMEM((members, 1, block, LANES), BF16),
            pltpu.VMEM((2, rows, LANES), BF16),
            pltpu.VMEM((rows, LANES), BF16),
            pltpu.VMEM((rows, LANES), BF16),
            pltpu.VMEM((LANES, rows), F32),
            pltpu.VMEM((members, 3, block, LANES), BF16),
            pltpu.VMEM((pairs, 3, block, LANES), BF16),
            pltpu.VMEM((2, block, width), BF16),
            pltpu.VMEM((3 * LANES, width), F32),
            pltpu.VMEM((2, members, held, 3 * LANES), BF16),
            pltpu.VMEM((2, members, held // 2, 3 * LANES), BF16),
            pltpu.VMEM((members, held // 2, 3 * LANES), BF16),
            pltpu.VMEM((pairs, held // 2, 3 * LANES), BF16),
            pltpu.VMEM((pairs, held, 3 * LANES), BF16),
            pltpu.VMEM((2, width, width), BF16),
            pltpu.VMEM((total, width), BF16),
            pltpu.VMEM((2, run, width), BF16),
            pltpu.VMEM((8, width), F32),
            pltpu.VMEM((8, width), F32),
            pltpu.VMEM((total, width), F32),
        ]
        + [pltpu.VMEM(found[0], BF16) for found in shapes]
        + [pltpu.VMEM(found[1], BF16) for found in shapes]
        + [pltpu.VMEM(shape, BF16) for found in shapes for shape in found[1:]]
        + [pltpu.VMEM((8, width), F32) for _ in vector_stages * 2]
        + [pltpu.VMEM((2, members, held // 2, 3 * LANES), BF16) for _ in range(grp_count - 1)]
        + [
            dma, dma((members,)), dma((members,)), dma((members,)), dma((members,)), dma((members,)), dma((members,)),
            dma((len(first),)), dma((len(first),)), dma((2,)), dma((2,)), dma((2,)), dma((2,)),
            dma((len(vector_stages),)), dma((len(vector_stages),)), dma((len(vector_stages),)),
            dma((len(vector_stages),)), dma, dma,
            dma((members,)), dma((pairs,)), dma((grp_count,)), dma((grp_count,)),
            dma((count, grps)), dma((count, grps)), dma((count,)), dma, dma, dma, dma,
        ]
        + [dma((count,)), dma((count,)), dma((count,)), dma((count, longest)), dma((count, longest))],
        compiler_params=pltpu.CompilerParams(
            vmem_limit_bytes=62 * 2**20, collective_id=collective_id, has_side_effects=True
        ),
        cost_estimate=pl.CostEstimate(
            flops=24 * rows * rows * LANES, bytes_accessed=64 * 2**20, transcendentals=2 * rows * rows
        ),
        name="backward",
    )(
        grad_blocks, qkv, key_aux, query, out_full, weight, start, grad_middle, gain.reshape(1, width),
        lead_rows, feed_vectors, up_vector, result.reshape(2, run, width), *first, *away, *stay,
    )


SMALL_ROWS = (0, 1, 2, 3, 4, 5, 8, 9, 10, 11)


def emit_kernel(
    bands, up_ref, down_ref, output_ref, heads_ref, own_grads_ref, other_grads_ref, result_ref,
    other_result_ref, late_ref, early_ref,
    up_out, down_out, output_out, heads_out, grads_out, result_out, up_vector_out, *small_outs,
):
    band = lax.axis_index("band")
    held = late_ref.shape[1] // bands
    half = band // (bands // 2)
    up_out[...] = up_ref[...].astype(F32)
    down_out[...] = down_ref[...].astype(F32)
    output_out[...] = output_ref[...].astype(F32)
    heads_out[...] = heads_ref[...].astype(F32)
    own, other = own_grads_ref[...], other_grads_ref[...].astype(F32)
    grads_out[0] = jnp.where(half == 0, own, other)
    grads_out[1] = jnp.where(half == 0, other, own)
    other = other_result_ref[...]
    result_out[0] = jnp.where(half == 0, result_ref[0], other)
    result_out[1] = jnp.where(half == 0, other, result_ref[1])

    @pl.when(pl.program_id(0) == 0)
    def _():
        size = late_ref.shape[1] // bands
        here = pl.ds(pl.multiple_of(band * held // LANES * LANES, LANES), LANES)
        both = jnp.concatenate([late_ref[:, here], early_ref[:, here]], 0)
        value = both[:, :size]
        for i in range(1, LANES // size):
            value = jnp.where(lax.rem(band, LANES // size) == i, both[:, i * size : (i + 1) * size], value)
        for i, out in enumerate(small_outs):
            out[...] = value[SMALL_ROWS[i] : SMALL_ROWS[i] + 1]
        columns = up_vector_out.shape[1]
        spread = late_ref.shape[1] // columns
        at = pl.ds(pl.multiple_of(lax.rem(band, spread) * columns, columns), columns)
        value = early_ref[4:5, at]
        for i in range(1, 4):
            value = jnp.where(band // spread == i, early_ref[4 + i : 5 + i, at], value)
        up_vector_out[...] = value


def emit(up, down, output, heads, own_grads, other_grads, result, other_result, late, early, bands):
    run, width = own_grads.shape
    size = width // bands
    columns = 4 * width // bands
    steps = 2
    by_rows = lambda shape: pl.BlockSpec(
        shape[:-2] + (shape[-2] // steps, shape[-1]), lambda i: (0,) * (len(shape) - 2) + (i, 0)
    )
    matrices = (up, down, output, heads)
    both = (2, run, width)
    return pl.pallas_call(
        functools.partial(emit_kernel, bands),
        grid=(steps,),
            in_specs=[by_rows(m.shape) for m in matrices]
            + [by_rows((run, width)), by_rows((run, width)), by_rows(both), by_rows((run, width))]
            + [constant(8, width)] * 2,
            out_specs=tuple(by_rows(m.shape) for m in matrices)
            + (by_rows(both), by_rows(both), constant(1, columns))
            + (constant(1, size),) * len(SMALL_ROWS),
        out_shape=tuple(jax.ShapeDtypeStruct(m.shape, F32) for m in matrices)
        + (
            jax.ShapeDtypeStruct(both, F32),
            jax.ShapeDtypeStruct(both, BF16),
            jax.ShapeDtypeStruct((1, columns), F32),
        )
        + (jax.ShapeDtypeStruct((1, size), F32),) * len(SMALL_ROWS),
        compiler_params=pltpu.CompilerParams(vmem_limit_bytes=VMEM_BYTES),
        cost_estimate=pl.CostEstimate(flops=0, bytes_accessed=8 * 2**20, transcendentals=0),
        name="emit",
    )(
        up, down, output, heads, own_grads, other_grads,
        result.reshape(both), other_result, late, early,
    )


def swap(array, stage):
    axis, bit = stage
    size = lax.axis_size(axis)
    return lax.ppermute(array, axis, [(i, i ^ (1 << bit)) for i in range(size)])


def bit_of(stage):
    axis, bit = stage
    return (lax.axis_index(axis) >> bit) & 1


def take(array, axis, index):
    return lax.dynamic_index_in_dim(array, index, axis, keepdims=False)


def after(value, *others):
    return lax.optimization_barrier((value,) + others)[0]


def bits(size):
    return size.bit_length() - 1


def local(
    tokens,
    lead_index,
    segment,
    valid,
    lead_weight,
    lead_bias,
    first_gain,
    first_shift,
    heads_weight,
    query_bias,
    value_bias,
    output_weight,
    output_bias,
    second_gain,
    second_shift,
    up_weight,
    up_bias,
    down_weight,
    down_bias,
    cotangent,
):
    bands, grps = lax.axis_size("band"), lax.axis_size("grp")
    groups, rows, width = tokens.shape
    total = groups * rows
    pairs = width // LANES
    members = bands // groups
    band = lax.axis_index("band")
    far = ("band", bits(bands) - 1)
    own_group = bit_of(far)
    block = total

    core = lax.rem(band, 2).astype(jnp.int32).reshape(1)
    qkv, attended, grad_out, start, first_low, lead_rows, key_aux, out_full, query_marked = forward(
        tokens, cotangent, lead_index, segment, valid, lead_weight, lead_bias, first_gain, first_shift,
        heads_weight, query_bias, value_bias, members, 1,
    )

    def normed_of(offset):
        return lax.ppermute(
            after(first_low, attended), "band", [(i, i ^ offset) for i in range(bands)]
        )

    first_rows = [first_low] + [normed_of(2 * k) for k in range(1, members // 2)]

    (
        result, grad_middle, grad_blocks, down_away, down_stay, up_away, up_stay,
        output_away, output_stay, feed_vectors, grad_up_bias,
    ) = feed(
        core, attended, start, grad_out, output_weight, output_bias, second_gain, second_shift,
        up_weight, up_bias, down_weight, down_bias, bands,
    )
    split = lambda v: v.reshape((2,) * (bits(bands) - 1) + v.shape[1:])
    held_up, held_down, inner = up_stay.shape[1], down_stay.shape[1], up_weight.shape[1]
    lead = [b for b in range(1, bits(bands))][::-1]

    def plan(array, rows_of, columns_of):
        return {"array": array, "rows": rows_of, "columns": columns_of, "lead": lead}

    quarter, fourth = inner // 4, held_down // 4
    plans = []
    for i in range(4):
        plans.append(plan(0, (0, held_up), (i * quarter, quarter)))
        plans.append(plan(1, (i * fourth, fourth), (0, width)))
    plans.append(plan(2, (0, held_up), (0, width)))
    grad_up, grad_down, grad_output, grad_heads, late, early, own_grads, other_grads, other_result, _ = backward(
        grad_blocks, qkv, key_aux, query_marked, out_full, first_rows, heads_weight, start, grad_middle,
        first_gain, lead_rows, feed_vectors, grad_up_bias, result,
        [split(v) for v in (up_away, down_away, output_away)],
        [split(v) for v in (up_stay, down_stay, output_stay)],
        plans, pairs, bands, grps, 3,
    )
    grad_up, grad_down, grad_output, grad_heads, grad_tokens, outcome, *vectors = emit(
        grad_up, grad_down, grad_output, grad_heads, own_grads, other_grads, result, other_result,
        late, early, bands,
    )
    grad_up_bias, *small = [v.reshape(-1) for v in vectors]
    return (
        outcome,
        grad_tokens,
        *small[:4],
        grad_heads,
        *small[4:6],
        grad_output,
        *small[6:9],
        grad_up,
        grad_up_bias,
        grad_down,
        small[9],
    )


def solution(mesh):
    rows = P("grp", "band", None)
    in_specs = (rows, P("grp", None), P("grp", None), P("grp", None)) + (P(),) * 15 + (rows,)
    vector, matrix = P("band"), P("band", None)
    out_specs = (
        rows,
        rows,
        vector,
        vector,
        vector,
        vector,
        matrix,
        vector,
        vector,
        matrix,
        vector,
        vector,
        vector,
        matrix,
        vector,
        matrix,
        vector,
    )
    return jax.shard_map(local, mesh=mesh, in_specs=in_specs, out_specs=out_specs, check_vma=False)
```

```python
import functools

import jax
import jax.numpy as jnp
from jax import lax
from jax.experimental import pallas as pl
from jax.experimental.pallas import tpu as pltpu
from jax.sharding import PartitionSpec as P

HEADS = 16
HEAD_DIM = 64
LANES = 128
MESH = pl.DeviceIdType.MESH
F32 = jnp.float32
BF16 = jnp.bfloat16
VMEM_BYTES = 56 * 2**20
MASKED = -1e30


def layer_norm(values, gain, shift):
    center = values - jnp.mean(values, -1, keepdims=True)
    spread = jnp.mean(center * center, -1, keepdims=True)
    return center * lax.rsqrt(spread + 1e-05) * gain + shift


def gelu_exact(values):
    return jax.nn.gelu(values, approximate=False)


def lane_of(shape):
    return lax.broadcasted_iota(jnp.int32, shape, 1)


def in_head(shape, head):
    return lane_of(shape) // HEAD_DIM == head


def spare_lane(shape, head):
    lane = lane_of(shape)
    return jnp.where(lane // HEAD_DIM == head, LANES, lane % HEAD_DIM)


def split_terms(column, spare):
    high = column.astype(BF16).astype(F32)
    middle = (column - high).astype(BF16).astype(F32)
    low = column - high - middle
    return (
        jnp.where(spare == 2, high, 0.0)
        + jnp.where(spare == 3, middle, 0.0)
        + jnp.where(spare == 4, low, 0.0)
    )


def dot_nt(left, right):
    return lax.dot_general(left, right, (((1,), (1,)), ((), ())), preferred_element_type=F32)


def dot_tn(left, right):
    return lax.dot_general(left, right, (((0,), (0,)), ((), ())), preferred_element_type=F32)


def dot_nn(left, right):
    return jnp.dot(left, right, preferred_element_type=F32)


def forward_kernel(
    block, members, pairs,
    tokens_ref, cotangent_ref, lead_ref, segment_ref, valid_ref, lead_weight_ref, lead_bias_ref, gain_ref, shift_ref,
    weight_ref, query_bias_ref, value_bias_ref,
    qkv_ref, attended_ref, grads_ref, start_ref, first_ref, lead_out_ref, key_aux_ref, out_full_ref, query_ref,
    tokens_s, weight_s, blocks_s, query_aux, segment_s, qkv_in, key_s, value_s, out_s,
    token_sem, swap_send, swap_recv, weight_sem, local_sem, keep_sem, qkv_send, qkv_recv, out_send, out_recv,
):
    rows = members * block
    run = block // 2
    width = start_ref.shape[1]
    scale = HEAD_DIM ** (-0.5)
    copies = members // pairs
    band, grp = lax.axis_index("band"), lax.axis_index("grp")
    me = lax.rem(band, members)
    base = band - me
    others = [lax.rem(me + i, members) for i in range(1, members)]
    half, far = flip("band", bits(members))

    barrier = pltpu.get_barrier_semaphore()
    greeted = [(base + other, grp) for other in others] + [far]
    for device in greeted:
        pl.semaphore_signal(barrier, inc=1, device_id=device, device_id_type=MESH)
    pl.semaphore_wait(barrier, len(greeted))

    def remote(source, target, send, recv, device):
        return pltpu.make_async_remote_copy(
            src_ref=source, dst_ref=target, send_sem=send, recv_sem=recv, device_id=device, device_id_type=MESH
        )

    tokens_swap = remote(tokens_ref.at[1 - half], tokens_s.at[1], swap_send.at[0], swap_recv.at[0], far)
    tokens_swap.start()
    own_tokens = pltpu.make_async_copy(tokens_ref.at[half], tokens_s.at[0], token_sem)
    own_tokens.start()
    own_run = pl.ds(pl.multiple_of(half * run, run), run)
    other_run = pl.ds(pl.multiple_of((1 - half) * run, run), run)

    def weight_load(t):
        return pltpu.make_async_copy(weight_ref.at[:, pl.ds(t * width, width)], weight_s.at[t], weight_sem.at[t])

    for t in (1, 2, 0):
        weight_load(t).start()

    def in_order(ref):
        value = jnp.where(half == 0, ref[0:1], ref[1:2])
        pieces = [
            value[:, (j + r * members) * run : (j + r * members + 1) * run] for j in range(members) for r in range(2)
        ]
        return jnp.concatenate(pieces, -1)

    segment, valid = in_order(segment_ref), in_order(valid_ref)
    segment_s[...] = segment
    place = lax.broadcasted_iota(jnp.int32, (8, rows), 0)
    hidden = lambda sample: jnp.where((segment == sample) & (valid == 1), 0.0, MASKED)
    feature = jnp.where(place == 0, hidden(0), jnp.where(place == 1, hidden(1), 0.0))
    feature = jnp.where(place == 2, 1.0, feature)
    feature = jnp.where(place == 3, (segment == 0).astype(F32), feature)
    feature = jnp.where(place == 4, (segment == 1).astype(F32), feature).astype(BF16)
    row = lax.broadcasted_iota(jnp.int32, (8, LANES), 0)
    spare = lax.broadcasted_iota(jnp.int32, (8, LANES), 1) % HEAD_DIM
    for_key = ((row < 2) & (spare == row)) | ((row == 2) & (spare >= 2) & (spare <= 4))
    for_query = (row >= 3) & (row <= 4) & (spare == row - 3)
    key_aux_ref[...] = dot_tn(feature, for_key.astype(BF16)).astype(BF16)
    query_aux[...] = dot_tn(feature, for_query.astype(BF16)).astype(BF16)
    days = lead_ref[...].astype(F32) * 0.25
    days = jnp.where(half == 0, days[0:1], days[1:2])
    own_segment = segment_s[:, pl.ds(pl.multiple_of(me * block, block), block)]
    lead = jnp.where(own_segment == 0, days[:, 0:1], days[:, 1:2])
    lead = jnp.where(lax.broadcasted_iota(jnp.int32, (8, block), 0) == 0, lead, 0.0).astype(BF16)
    lead_out_ref[...] = dot_tn(lead, (row == 0).astype(BF16))

    def qkv_copy(t, phase, i, other):
        here = own_run if phase == 0 else other_run
        return remote(
            blocks_s.at[other // copies, t, here],
            qkv_in.at[me, t, here],
            qkv_send.at[t, phase, i],
            qkv_recv.at[t, phase, i],
            (base + other, grp),
        )

    def project(phase):
        here = own_run if phase == 0 else other_run
        lead_here = jnp.concatenate([lead_out_ref[here]] * (width // LANES), -1)
        start = tokens_s[phase].astype(F32) + lead_here * lead_weight_ref[...] + lead_bias_ref[...]
        start_ref[here] = start
        first = (normalised(start)[0] * gain_ref[...] + shift_ref[...]).astype(BF16)
        first_ref[here] = first
        for t in (1, 2, 0):
            if phase == 0:
                weight_load(t).wait()
            joined = dot_nn(first, weight_s[t])
            if t != 1:
                joined = joined + (query_bias_ref if t == 0 else value_bias_ref)[...]
            joined = joined.astype(BF16)
            for pair in range(pairs):
                blocks_s[pair, t, here] = joined[:, pair * LANES : (pair + 1) * LANES]
            for i, other in enumerate(others):
                qkv_copy(t, phase, i, other).start()
            qkv_in[me, t, here] = blocks_s[me // copies, t, here]

    own_tokens.wait()
    project(0)
    tokens_swap.wait_recv()
    grads_swap = remote(cotangent_ref.at[1 - half], grads_ref.at[own_run], swap_send.at[1], swap_recv.at[1], far)
    grads_own = pltpu.make_async_copy(cotangent_ref.at[half], grads_ref.at[own_run], local_sem)
    project(1)
    grads_own.start()

    for i, other in enumerate(others):
        for phase in range(2):
            qkv_copy(1, phase, i, other).wait_recv()
    keys = qkv_in[:, 1].reshape(rows, LANES)
    for head in range(2):
        key_s[head] = jnp.where(in_head(keys.shape, head), keys, key_aux_ref[...])
    for i, other in enumerate(others):
        for phase in range(2):
            qkv_copy(2, phase, i, other).wait_recv()
    value_s[...] = qkv_in[:, 2].reshape(rows, LANES)
    keep = pltpu.make_async_copy(qkv_in.at[:, pl.ds(1, 2)], qkv_ref.at[:, pl.ds(1, 2)], keep_sem)
    keep.start()

    def sends_to(other):
        return (lax.rem(other, copies) == lax.rem(me, copies)) & (other != me)

    def out_copy(other):
        return remote(
            out_s.at[other],
            attended_ref.at[me // copies],
            out_send.at[other // copies],
            out_recv.at[me // copies],
            (base + other, grp),
        )

    @pl.loop(0, members)
    def _(i):
        other = lax.rem(me + members - i, members)

        @pl.when(i > 0)
        def _():
            for phase, here in enumerate((own_run, other_run)):
                landed = qkv_in.at[other, 0, here]
                pltpu.make_async_copy(landed, landed, qkv_recv.at[0, phase, i - 1]).wait()

        here = pl.ds(pl.multiple_of(other * block, block), block)
        query = qkv_in[other, 0].astype(F32) * scale
        aux = query_aux[here].astype(F32)
        shape = query.shape
        mixed = []
        for head in range(2):
            inside = in_head(shape, head)
            marked = jnp.where(inside, query, aux)
            scores = dot_nt(marked.astype(BF16), key_s[head])
            peak = jnp.max(scores, -1, keepdims=True)
            weights = jnp.exp(scores - peak)
            total = jnp.sum(weights, -1, keepdims=True)
            mixed.append(dot_nn(weights.astype(BF16), value_s[...]) / total)
            logsum = peak + jnp.log(total)
            marked = marked + split_terms(-logsum, spare_lane(shape, head))
            query_ref[head, here] = marked.astype(BF16)
        both = jnp.where(in_head(shape, 0), mixed[0], mixed[1])
        out_full_ref[here] = both
        out_s[other, 0] = both.astype(BF16)

        @pl.when(sends_to(other))
        def _():
            out_copy(other).start()

        @pl.when(i == 0)
        def _():
            grads_swap.start()

    own_out = pltpu.make_async_copy(out_s.at[me], attended_ref.at[me // copies], token_sem)
    own_out.start()
    queries = pltpu.make_async_copy(qkv_in.at[:, 0], qkv_ref.at[:, 0], local_sem)
    keep.wait()
    own_out.wait()
    grads_own.wait()
    queries.start()
    queries.wait()
    tokens_swap.wait_send()
    for t in range(3):
        for phase in range(2):
            for i, other in enumerate(others):
                qkv_copy(t, phase, i, other).wait_send()
    for other in others:

        @pl.when(sends_to(other))
        def _():
            out_copy(other).wait_send()

    for i in range(1, pairs):
        slot = lax.rem(me // copies + i, pairs)
        pltpu.make_async_copy(attended_ref.at[slot], attended_ref.at[slot], out_recv.at[slot]).wait()
    grads_swap.wait_send()
    pltpu.make_async_copy(grads_ref.at[other_run], grads_ref.at[other_run], swap_recv.at[1]).wait()


def forward(
    tokens, cotangent, lead_index, segment, valid, lead_weight, lead_bias, gain, shift, weight, query_bias,
    value_bias, members, collective_id,
):
    _, run, width = tokens.shape
    block = 2 * run
    rows = members * block
    pairs = width // LANES
    row = lambda v: v.reshape(1, width)
    vmem = pl.BlockSpec(memory_space=pltpu.VMEM)
    anywhere = pl.BlockSpec(memory_space=pl.ANY)
    dma = pltpu.SemaphoreType.DMA
    return pl.pallas_call(
        functools.partial(forward_kernel, block, members, pairs),
        out_shape=(
            jax.ShapeDtypeStruct((members, 3, block, LANES), BF16),
            jax.ShapeDtypeStruct((pairs, 1, block, LANES), BF16),
            jax.ShapeDtypeStruct((block, width), BF16),
            jax.ShapeDtypeStruct((block, width), F32),
            jax.ShapeDtypeStruct((block, width), BF16),
            jax.ShapeDtypeStruct((block, LANES), F32),
            jax.ShapeDtypeStruct((rows, LANES), BF16),
            jax.ShapeDtypeStruct((rows, LANES), F32),
            jax.ShapeDtypeStruct((2, rows, LANES), BF16),
        ),
        in_specs=[anywhere, anywhere] + [vmem] * 7 + [anywhere, vmem, vmem],
        out_specs=(anywhere, anywhere, anywhere) + (vmem,) * 6,
        scratch_shapes=[
            pltpu.VMEM((2, run, width), BF16),
            pltpu.VMEM((3, width, width), BF16),
            pltpu.VMEM((pairs, 3, block, LANES), BF16),
            pltpu.VMEM((rows, LANES), BF16),
            pltpu.VMEM((1, rows), jnp.int32),
            pltpu.VMEM((members, 3, block, LANES), BF16),
            pltpu.VMEM((2, rows, LANES), BF16),
            pltpu.VMEM((rows, LANES), BF16),
            pltpu.VMEM((members, 1, block, LANES), BF16),
            dma, dma((2,)), dma((2,)), dma((3,)), dma, dma,
            dma((3, 2, members)), dma((3, 2, members)), dma((members,)), dma((members,)),
        ],
        compiler_params=pltpu.CompilerParams(
            vmem_limit_bytes=VMEM_BYTES, collective_id=collective_id, has_side_effects=True
        ),
        cost_estimate=pl.CostEstimate(
            flops=8 * rows * rows * LANES, bytes_accessed=32 * 2**20, transcendentals=2 * rows * rows
        ),
        name="forward",
    )(
        tokens, cotangent, lead_index, segment, valid, row(lead_weight), row(lead_bias), row(gain), row(shift),
        weight, row(query_bias), row(value_bias),
    )


def device_at(axis, index):
    band, grp = lax.axis_index("band"), lax.axis_index("grp")
    return (index, grp) if axis == "band" else (band, index)


def flip(axis, bit):
    index = lax.axis_index(axis)
    mine = lax.rem(index // (1 << bit), 2)
    return mine, device_at(axis, index + (1 - 2 * mine) * (1 << bit))


def normalised(values):
    center = values - jnp.mean(values, -1, keepdims=True)
    spread = jnp.mean(center * center, -1, keepdims=True)
    inverse = lax.rsqrt(spread + 1e-05)
    return center * inverse, inverse


def norm_backward(grads, gain, unit, inverse):
    inner = grads * gain
    at_input = inverse * (
        inner
        - jnp.mean(inner, -1, keepdims=True)
        - unit * jnp.mean(inner * unit, -1, keepdims=True)
    )
    return at_input, jnp.sum(grads * unit, 0, keepdims=True), jnp.sum(grads, 0, keepdims=True)


def by_core(value, core, held, away_ref, stay_ref):
    split = value.astype(BF16).reshape(-1, 2, held, value.shape[-1])
    even, odd = split[:, 0], split[:, 1]
    away_ref[...] = jnp.where(core == 0, odd, even)
    stay_ref[...] = jnp.where(core == 0, even, odd)


def constant(*shape):
    return pl.BlockSpec(shape, lambda *i: (0,) * len(shape))


def feed_kernel(
    core_ref, attended_ref, start_ref, grad_ref, output_weight_ref, output_bias_ref, gain_ref, shift_ref,
    up_ref, up_bias_ref, down_ref, down_bias_ref,
    result_ref, grad_middle_ref, grad_attended_ref, down_away, down_stay, up_away, up_stay,
    output_away, output_stay, vectors_ref, up_vector_ref,
    attended_s, middle_s, unit_s, inverse_s, second_s, second_turned, result_s, grad_second_s,
):
    step, steps = pl.program_id(0), pl.num_programs(0)
    core = core_ref[0]
    pairs = attended_ref.shape[0]

    @pl.when(step == 0)
    def _():
        for pair in range(pairs):
            attended_s[:, pair * LANES : (pair + 1) * LANES] = attended_ref[pair, 0]
        middle = (
            start_ref[...] + dot_nn(attended_s[...], output_weight_ref[...]) + output_bias_ref[...]
        )
        middle_s[...] = middle
        unit, inverse = normalised(middle)
        unit_s[...] = unit
        inverse_s[...] = inverse
        second = unit * gain_ref[...] + shift_ref[...]
        second_s[...] = second.astype(BF16)
        second_turned[...] = second.T.astype(BF16)
        result_s[...] = jnp.zeros_like(result_s)
        grad_second_s[...] = jnp.zeros_like(grad_second_s)

    grads = grad_ref[...]
    upper = dot_nn(second_s[...], up_ref[...]) + up_bias_ref[...]
    level = 0.5 + 0.5 * lax.erf(upper * 0.7071067811865476)
    hidden = (upper * level).astype(BF16)
    slope = level + upper * (0.3989422804014327 * jnp.exp(-0.5 * upper * upper))
    result_s[...] += dot_nn(hidden, down_ref[...])
    by_core(dot_tn(hidden, grads), core, down_away.shape[1], down_away, down_stay)
    grad_upper_wide = dot_nt(grads, down_ref[...]) * slope
    grad_upper = grad_upper_wide.astype(BF16)
    up_vector_ref[...] = jnp.sum(grad_upper.astype(F32), 0, keepdims=True)
    by_core(dot_nn(second_turned[...], grad_upper), core, up_away.shape[1], up_away, up_stay)
    grad_second_s[...] += dot_nt(grad_upper, up_ref[...])

    @pl.when(step == steps - 1)
    def _():
        result_ref[...] = (middle_s[...] + result_s[...] + down_bias_ref[...]).astype(BF16)
        wide = grads.astype(F32)
        at_input, grad_gain, grad_shift = norm_backward(
            grad_second_s[...], gain_ref[...], unit_s[...], inverse_s[...]
        )
        grad_middle = at_input + wide
        grad_middle_ref[...] = grad_middle
        branch = grad_middle.astype(BF16)
        by_core(dot_tn(attended_s[...], branch), core, output_away.shape[1], output_away, output_stay)
        grad_attended = dot_nt(branch, output_weight_ref[...]).astype(BF16)
        for pair in range(pairs):
            grad_attended_ref[pair, 0] = grad_attended[:, pair * LANES : (pair + 1) * LANES]
        vectors_ref[0:1] = jnp.sum(branch.astype(F32), 0, keepdims=True)
        vectors_ref[1:2] = grad_gain
        vectors_ref[2:3] = grad_shift
        vectors_ref[3:4] = jnp.sum(wide, 0, keepdims=True)


def feed(core, attended, start, grads, output_weight, output_bias, gain, shift, up, up_bias, down, down_bias, bands):
    total, width = start.shape
    inner = up.shape[1]
    pairs = width // LANES
    chunk = 1024
    held, held_down = width // bands, inner // bands
    per_chunk = chunk // held_down // 2
    row = lambda v: v.reshape(1, -1)
    half = bands // 2
    one = lambda *shape: constant(*shape)
    return pl.pallas_call(
        feed_kernel,
        grid_spec=pltpu.PrefetchScalarGridSpec(
            num_scalar_prefetch=1,
            grid=(inner // chunk,),
            in_specs=[
                one(pairs, 1, total, LANES),
                one(total, width),
                one(total, width),
                one(width, width),
                one(1, width),
                one(1, width),
                one(1, width),
                pl.BlockSpec((width, chunk), lambda j, c: (0, j)),
                pl.BlockSpec((1, chunk), lambda j, c: (0, j)),
                pl.BlockSpec((chunk, width), lambda j, c: (j, 0)),
                one(1, width),
            ],
            out_specs=(
                one(total, width),
                one(total, width),
                one(pairs, 1, total, LANES),
                pl.BlockSpec((per_chunk, held_down, width), lambda j, c: (j, 0, 0)),
                pl.BlockSpec((per_chunk, held_down, width), lambda j, c: (j, 0, 0)),
                pl.BlockSpec((half, held, chunk), lambda j, c: (0, 0, j)),
                pl.BlockSpec((half, held, chunk), lambda j, c: (0, 0, j)),
                one(half, held, width),
                one(half, held, width),
                one(8, width),
                pl.BlockSpec((1, chunk), lambda j, c: (0, j)),
            ),
            scratch_shapes=[
                pltpu.VMEM((total, width), BF16),
                pltpu.VMEM((total, width), F32),
                pltpu.VMEM((total, width), F32),
                pltpu.VMEM((total, 1), F32),
                pltpu.VMEM((total, width), BF16),
                pltpu.VMEM((width, total), BF16),
                pltpu.VMEM((total, width), F32),
                pltpu.VMEM((total, width), F32),
            ],
        ),
        out_shape=(
            jax.ShapeDtypeStruct((total, width), BF16),
            jax.ShapeDtypeStruct((total, width), F32),
            jax.ShapeDtypeStruct((pairs, 1, total, LANES), BF16),
            jax.ShapeDtypeStruct((half, held_down, width), BF16),
            jax.ShapeDtypeStruct((half, held_down, width), BF16),
            jax.ShapeDtypeStruct((half, held, inner), BF16),
            jax.ShapeDtypeStruct((half, held, inner), BF16),
            jax.ShapeDtypeStruct((half, held, width), BF16),
            jax.ShapeDtypeStruct((half, held, width), BF16),
            jax.ShapeDtypeStruct((8, width), F32),
            jax.ShapeDtypeStruct((1, inner), F32),
        ),
        compiler_params=pltpu.CompilerParams(vmem_limit_bytes=VMEM_BYTES),
        cost_estimate=pl.CostEstimate(
            flops=12 * total * width * inner, bytes_accessed=8 * width * inner, transcendentals=2 * total * inner
        ),
        name="feed",
    )(
        core, attended, start, grads, output_weight, row(output_bias), row(gain), row(shift),
        up, row(up_bias), down, row(down_bias),
    )


LINK = 26.0
CORE = 1.55
ADD = 0.4
HOP = 4.0


def plan_steps(sizes, stages, vector_stages, iterations, iteration, slack, late_slack):
    free = {link: 0.0 for link in ("x", "y", "z", "Z", "core")}
    held, left, orders = list(sizes), [list(stages) for _ in sizes], [[] for _ in sizes]
    ready, waiting, steps, count = [], [], [], 0
    now = 3.0

    def occupy(link, size):
        if link == "Z":
            free["Z"] = max(now, free["Z"]) + 2 * size * LINK
            free["z"] = max(now, free["z"]) + size * LINK
        else:
            free[link] = max(now, free[link]) + size * (CORE if link == "core" else LINK)
        return free[link] + HOP

    def expect(arrival, name, argument=None):
        nonlocal count
        count += 1
        waiting.append((arrival, count, name, argument))

    def send_ready(limit):
        sent = True
        while sent:
            sent = False
            for link in sorted("xyzZ", key=lambda l: free[l]):
                fit = [
                    k
                    for k in ready
                    if any(stages[s] == link for s in left[k])
                    and (link != "Z" or len(orders[k]) >= len(stages) - 1)
                ]
                if free[link] - now >= limit or not fit:
                    continue
                k = max(fit, key=lambda k: len(left[k]))
                stage = [s for s in left[k] if stages[s] == link][0]
                left[k].remove(stage)
                orders[k].append(stage)
                held[k] /= 2
                ready.remove(k)
                steps.append(("send", k))
                expect(occupy(link, held[k]), "take", k)
                sent = True
                break

    def vector_hop(name, hop):
        if hop < len(vector_stages):
            expect(occupy(stages.get(vector_stages[hop], "core"), 0.035), name, hop)

    def perform(name, argument):
        nonlocal now
        steps.append((name, argument))
        if name == "take":
            k = argument
            now += held[k] * ADD + 0.1
            if left[k]:
                ready.append(k)
            else:
                occupy("y", held[k])
        elif name in ("early", "late"):
            now += 0.2
            vector_hop(name, argument + 1)
        elif name == "grads":
            now += 3.0
            expect(now, "iteration", 0)
        elif name == "iteration":
            now += iteration
            for link in "xz":
                occupy(link, 0.5 / iterations)
            if argument + 1 < iterations:
                expect(now, "iteration", argument + 1)
            else:
                expect(now, "queries")
        elif name == "queries":
            now += 2.0
            expect(max(occupy("x", 0.25), occupy("z", 0.25)), "joined")
            expect(now, "products")
        elif name == "products":
            now += 4.5
            expect(occupy("y", 0.19), "near")
        elif name == "joined":
            now += 5.0
            expect(now, "start")
        elif name == "start":
            now += 3.0
            occupy("Z", 0.25)
            vector_hop("late", 0)
        elif name == "near":
            now += 0.3
            expect(occupy("Z", 0.1), "far")
        elif name == "far":
            now += 0.3
            expect(max(occupy("x", 0.06), occupy("z", 0.06)), "members")
        elif name == "members":
            now += 0.3
            expect(occupy("y", 0.1), "rows")
        elif name == "rows":
            now += 0.5

    expect(max(occupy("x", 0.25), occupy("z", 0.25)), "grads")
    for k, size in enumerate(sizes):
        expect(occupy("core", size), "take", k)
    occupy("Z", 0.25)
    vector_hop("early", 0)
    main = ("grads", "iteration", "queries", "products", "joined", "start")
    while waiting or ready:
        if not waiting:
            send_ready(1e9)
        arrived = [w for w in waiting if w[0] <= now]
        others = [w for w in arrived if w[2] not in main]
        chosen = min(others or arrived or waiting)
        waiting.remove(chosen)
        now = max(now, chosen[0])
        perform(*chosen[2:])
        looped = any(w[2] in ("grads", "iteration") for w in waiting)
        send_ready(slack if looped else late_slack)
    return orders, steps, now, free


class Flow:
    def __init__(self, k, plan, away, stay, core_in, stay_s, buffers, sems):
        self.k, self.plan, self.away, self.stay = k, plan, away, stay
        self.core_in, self.stay_s, self.buffers = core_in, stay_s, buffers
        self.core_send, self.core_recv, self.stay_sem, self.send_sem, self.recv_sem = sems
        self.stages, self.lead = plan["stages"], list(plan["lead"])
        self.flips = [flip(*stage) for stage in self.stages]
        self.core_other = flip("band", 0)[1]
        self.held, self.at = None, -1

    @staticmethod
    def shapes(plan):
        shape, lead = [2] * len(plan["lead"]) + [plan["rows"][1], plan["columns"][1]], list(plan["lead"])
        found = [tuple(shape)]
        for axis, bit in plan["stages"]:
            if axis == "band":
                at = lead.index(bit)
                del shape[at], lead[at]
            else:
                shape[-1] //= 2
            found.append(tuple(shape))
        return found

    def region(self, stage, index):
        (first, rows), (column, columns) = self.plan["rows"], self.plan["columns"]
        where = [slice(None)] * len(self.plan["lead"]) + [pl.ds(first, rows), pl.ds(column, columns)]
        if stage is not None:
            axis, bit = stage
            if axis == "band":
                where[self.plan["lead"].index(bit)] = index
            else:
                half = columns // 2
                where[-1] = pl.ds(pl.multiple_of(column + index * half, LANES), half)
        return tuple(where)

    def pick(self, ref, index):
        axis, bit = self.stages[self.at]
        where = [slice(None)] * len(ref.shape)
        if axis == "band":
            where[self.lead.index(bit)] = index
        else:
            half = ref.shape[-1] // 2
            where[-1] = pl.ds(pl.multiple_of(index * half, LANES), half)
        return tuple(where)

    def core_copy(self):
        return pltpu.make_async_remote_copy(
            src_ref=self.away.at[self.region(None, None)],
            dst_ref=self.core_in,
            send_sem=self.core_send.at[self.k],
            recv_sem=self.core_recv.at[self.k],
            device_id=self.core_other,
            device_id_type=MESH,
        )

    def stay_copy(self, index):
        return pltpu.make_async_copy(
            self.stay.at[self.region(self.stages[0], index)], self.stay_s, self.stay_sem.at[self.k]
        )

    def stage_copy(self, stage, source):
        return pltpu.make_async_remote_copy(
            src_ref=source,
            dst_ref=self.buffers[stage],
            send_sem=self.send_sem.at[self.k, stage],
            recv_sem=self.recv_sem.at[self.k, stage],
            device_id=self.flips[stage][1],
            device_id_type=MESH,
        )

    def start(self):
        self.core_copy().start()
        self.stay_copy(1 - self.flips[0][0]).start()

    def take(self):
        if self.at < 0:
            self.at = 0
            mine = self.flips[0][0]
            self.core_copy().wait_recv()
            self.stay_copy(1 - mine).wait()
            away = self.pick(self.core_in, 1 - mine)
            self.core_in[away] = self.core_in[away] + self.stay_s[...]
            self.stay_copy(mine).start()
            self.held = self.core_in
            return False
        mine = self.flips[self.at][0]
        buffer = self.buffers[self.at]
        self.stage_copy(self.at, buffer).wait_recv()
        kept = self.held[self.pick(self.held, mine)]
        if self.at == 0:
            self.stay_copy(mine).wait()
            kept = kept + self.stay_s[...]
        buffer[...] = buffer[...] + kept
        axis, bit = self.stages[self.at]
        if axis == "band":
            self.lead.remove(bit)
        self.held = buffer
        self.at += 1
        return self.at == len(self.stages)

    def send(self):
        self.stage_copy(self.at, self.held.at[self.pick(self.held, 1 - self.flips[self.at][0])]).start()

    def drain(self):
        self.core_copy().wait_send()
        for stage, buffer in enumerate(self.buffers):
            self.stage_copy(stage, buffer).wait_send()


class FullFlow:
    def __init__(self, held, stages, buffers, send_sem, recv_sem):
        self.held, self.stages, self.buffers = held, stages, buffers
        self.send_sem, self.recv_sem = send_sem, recv_sem
        self.flips = [flip(*stage) for stage in stages]
        self.at = 0

    def copy(self, stage, source):
        return pltpu.make_async_remote_copy(
            src_ref=source,
            dst_ref=self.buffers[stage],
            send_sem=self.send_sem.at[stage],
            recv_sem=self.recv_sem.at[stage],
            device_id=self.flips[stage][1],
            device_id_type=MESH,
        )

    def send(self):
        if self.at < len(self.stages):
            self.copy(self.at, self.held).start()

    def step(self):
        if self.at < len(self.stages):
            buffer = self.buffers[self.at]
            self.copy(self.at, buffer).wait_recv()
            buffer[...] = buffer[...] + self.held[...]
            self.held = buffer
            self.at += 1
            self.send()

    def drain(self):
        for stage, buffer in enumerate(self.buffers):
            self.copy(stage, buffer).wait_send()


def backward_kernel(
    block, members, pairs, grps, plans, steps, vector_stages,
    grad_ref, qkv_ref, key_aux_ref, query_ref, out_full_ref, weight_ref, start_ref, grad_middle_ref, gain_ref, lead_ref, feed_ref, up_vector_ref, result_ref, *refs,
):
    count = len(plans)
    arrays = max(plan["array"] for plan in plans) + 1
    refs = list(refs)
    firsts = members // 2

    def grab(n):
        found = refs[:n]
        del refs[:n]
        return found

    first_refs, away_refs, stay_refs = grab(firsts), grab(arrays), grab(arrays)
    up_ref, down_ref, output_ref, heads_ref, late_ref, early_ref = grab(6)
    own_tokens_ref, other_tokens_ref, other_result_ref, first_other = grab(4)
    grad_in, grad_s, query_s, plain_s, query_sum, out_s, joined_in = grab(7)
    normed_s, heads_s, heads_in, heads_near, heads_got, heads_sum, heads_rows = grab(7)
    weight_s, joined_s, tokens_s, late_s, early_s, grad_first = grab(6)
    core_in, stay_s = grab(count), grab(count)
    buffers = [grab(len(plan["stages"])) for plan in plans]
    late_buffers, early_buffers = grab(len(vector_stages)), grab(len(vector_stages))
    grp_count = bits(grps)
    heads_buffers = grab(grp_count - 1)
    (
        local_sem, grad_send, grad_recv, out_send, out_recv, query_send, query_recv, first_send, first_recv,
        normed_sem, weight_sem, swap_send, swap_recv, late_send, late_recv, early_send, early_recv, far_send, far_recv,
        heads_send, heads_recv, heads_two_send, heads_two_recv, gather_send, gather_recv, own_sem,
        near_send, near_recv, rows_send, rows_recv,
    ) = grab(30)
    flow_sems = grab(5)

    rows = key_aux_ref.shape[0]
    width = start_ref.shape[1]
    scale = HEAD_DIM ** (-0.5)
    copies = members // pairs
    band, grp = lax.axis_index("band"), lax.axis_index("grp")
    me = lax.rem(band, members)
    base = band - me
    others = [lax.rem(me + i, members) for i in range(1, members)]
    groups_off = [lax.rem(grp + i, grps) for i in range(1, grps)]
    half, far = flip("band", bits(members))
    core_other = flip("band", 0)[1]
    flows = [
        Flow(k, plan, away_refs[plan["array"]], stay_refs[plan["array"]], core_in[k], stay_s[k], buffers[k], flow_sems)
        for k, plan in enumerate(plans)
    ]
    late = FullFlow(late_s, vector_stages, late_buffers, late_send, late_recv)
    early = FullFlow(early_s, vector_stages, early_buffers, early_send, early_recv)
    heads_flow = FullFlow(
        heads_near, [("grp", b) for b in range(1, grp_count)], heads_buffers, heads_two_send, heads_two_recv
    )
    near_mine, near = flip("grp", 0)
    near_rows = heads_near.shape[2]
    own_rows = pl.ds(pl.multiple_of(near_mine * near_rows, near_rows), near_rows)
    sent_rows = pl.ds(pl.multiple_of((1 - near_mine) * near_rows, near_rows), near_rows)

    barrier = pltpu.get_barrier_semaphore()
    greeted = [(base + other, grp) for other in others] + [(band, g) for g in groups_off] + [far]
    for device in greeted:
        pl.semaphore_signal(barrier, inc=1, device_id=device, device_id_type=MESH)
    pl.semaphore_wait(barrier, len(greeted))

    def remote(source, target, send, recv, device):
        return pltpu.make_async_remote_copy(
            src_ref=source, dst_ref=target, send_sem=send, recv_sem=recv, device_id=device, device_id_type=MESH
        )

    grad_copies = [
        remote(
            grad_ref.at[other // copies], grad_in.at[me], grad_send.at[i], grad_recv.at[i], (base + other, grp)
        )
        for i, other in enumerate(others)
    ]
    for copy in grad_copies:
        copy.start()
    own = pltpu.make_async_copy(grad_ref.at[me // copies], grad_in.at[me], local_sem)
    own.start()
    for flow in flows:
        flow.start()
    first_copies = [
        remote(first_refs[k], first_other.at[k], first_send.at[k], first_recv.at[k], core_other) for k in range(firsts)
    ]
    for copy in first_copies:
        copy.start()
    result_copy = remote(result_ref.at[1 - half], other_result_ref, swap_send.at[0], swap_recv.at[0], far)
    result_copy.start()

    def weight_load(t):
        return pltpu.make_async_copy(
            weight_ref.at[:, pl.ds(t * width, width)], weight_s.at[t % 2], weight_sem.at[t % 2]
        )

    for t in range(2):
        weight_load(t).start()
    early_s[0:4] = feed_ref[0:4]
    for i in range(4):
        early_s[4 + i : 5 + i] = up_vector_ref[:, i * width : (i + 1) * width]
    early.send()
    query_s[...] = qkv_ref[:, 0].reshape(rows, LANES)
    query_sum[...] = jnp.zeros_like(query_sum)

    gathers = []

    def gather_copies(k):
        plan, flow = plans[k], flows[k]
        target = (up_ref, down_ref, output_ref)[plan["array"]]
        size = plan["columns"][1]
        columns = size >> grp_count
        offset = plan["columns"][0]
        for b in range(grp_count):
            size //= 2
            offset = offset + flip("grp", b)[0] * size
        where = target.at[pl.ds(*plan["rows"]), pl.ds(pl.multiple_of(offset, LANES), columns)]
        held = flow.buffers[-1]
        mine = pltpu.make_async_copy(held, where, own_sem.at[k])
        return [mine] + [
            remote(held, where, gather_send.at[k, i], gather_recv.at[k, i], (band, g))
            for i, g in enumerate(groups_off)
        ]

    slots = [[]]
    for step in steps:
        if step[0] in ("grads", "iteration", "queries"):
            slots.append([])
        else:
            slots[-1].append(step)
    rest = slots.pop()

    def small_step(name, argument):
        if name == "send":
            flows[argument].send()
        elif name == "early":
            early.step()
        elif name == "late":
            late.step()
        elif flows[argument].take():
            for copy in gather_copies(argument):
                copy.start()

    def advance(slot):
        for step in slots[slot]:
            small_step(*step)

    advance(0)
    own.wait()
    for copy in grad_copies:
        copy.wait_recv()
    grads = grad_in[...].reshape(rows, LANES)
    plain_s[...] = grads
    wide = grads.astype(F32)
    product = wide * out_full_ref[...]
    for head in range(2):
        inside = in_head(wide.shape, head)
        delta = jnp.sum(jnp.where(inside, product, 0.0), -1, keepdims=True)
        marked = jnp.where(inside, wide, split_terms(-delta, spare_lane(wide.shape, head)))
        grad_s[head] = marked.astype(BF16)

    def sends_to(other):
        return (lax.rem(other, copies) == lax.rem(me, copies)) & (other != me)

    def out_copy(other):
        return remote(
            out_s.at[other, pl.ds(1, 2)],
            joined_in.at[me // copies, pl.ds(1, 2)],
            out_send.at[other // copies],
            out_recv.at[me // copies],
            (base + other, grp),
        )

    def query_copy(other):
        return remote(
            out_s.at[other, 0],
            joined_in.at[me // copies, 0],
            query_send.at[other // copies],
            query_recv.at[me // copies],
            (base + other, grp),
        )

    sub = min(block, 2**19 // rows)

    @pl.loop(0, members)
    def _(i):
        for slot in range(1, 1 + members):
            if slots[slot]:

                @pl.when(i == slot - 1)
                def _(slot=slot):
                    advance(slot)

        other = lax.rem(me + 1 + i, members)
        for low in range(0, block, sub):
            here = pl.ds(pl.multiple_of(other * block + low, sub), sub)
            key = qkv_ref[other, 1, pl.ds(low, sub)]
            value = qkv_ref[other, 2, pl.ds(low, sub)]
            aux = key_aux_ref[here]
            shape = key.shape
            grad_key, grad_value = [], []
            for head in range(2):
                inside = in_head(shape, head)
                spare = spare_lane(shape, head)
                ones = jnp.where((spare >= 2) & (spare <= 4), 1.0, 0.0).astype(BF16)
                probs = jnp.exp(dot_nt(jnp.where(inside, key, aux), query_ref[head]))
                grad_probs = dot_nt(jnp.where(inside, value, ones), grad_s[head])
                grad_scores = (probs * grad_probs).astype(BF16)
                grad_value.append(dot_nn(probs.astype(BF16), plain_s[...]))
                grad_key.append(dot_nn(grad_scores, query_s[...]))
                query_sum[...] += dot_tn(jnp.where(inside, key, jnp.zeros_like(key)), grad_scores)
            first = in_head(shape, 0)
            out_s[other, 1, pl.ds(low, sub)] = (jnp.where(first, grad_key[0], grad_key[1]) * scale).astype(BF16)
            out_s[other, 2, pl.ds(low, sub)] = jnp.where(first, grad_value[0], grad_value[1]).astype(BF16)

        @pl.when(sends_to(other))
        def _():
            out_copy(other).start()

    advance(members + 1)
    out_s[:, 0] = (query_sum[...].T * scale).astype(BF16).reshape(members, block, LANES)
    for other in others:

        @pl.when(sends_to(other))
        def _():
            query_copy(other).start()

    joined_in[me // copies] = out_s[me]

    def normed_load(i):
        source = first_refs[i // 2] if i % 2 == 0 else first_other.at[i // 2]
        return pltpu.make_async_copy(source, normed_s.at[i % 2], normed_sem.at[i % 2])

    def near_copy():
        return remote(heads_in.at[:, :, sent_rows], heads_near, near_send, near_recv, near)

    def far_copy():
        return remote(heads_flow.held.at[1 - half], heads_got, far_send, far_recv, far)

    def tokens_copy():
        return remote(tokens_s.at[1 - half], other_tokens_ref, swap_send.at[1], swap_recv.at[1], far)

    def heads_copy(i, other):
        return remote(
            heads_got.at[other], heads_sum.at[me // copies], heads_send.at[i], heads_recv.at[me // copies],
            (base + other, grp),
        )

    def rows_copy():
        return remote(heads_sum, heads_rows.at[:, own_rows], rows_send, rows_recv, near)

    def products_step():
        for copy in first_copies:
            copy.wait_recv()
        normed_load(0).start()
        for i in range(members):
            if i + 1 < members:
                normed_load(i + 1).start()
            rows_of = out_s[me ^ i]
            rows_of = jnp.concatenate([rows_of[t] for t in range(3)], -1)
            normed_load(i).wait()
            term = dot_tn(rows_of, normed_s[i % 2])
            heads_s[...] = term if i == 0 else heads_s[...] + term
        whole = heads_s[...].T.astype(BF16).reshape(heads_in.shape)
        heads_in[...] = jnp.where(lax.rem(me, copies) == 0, whole, jnp.zeros_like(whole))
        near_copy().start()

    def joined_step():
        for i in range(1, pairs):
            place = lax.rem(me // copies + i, pairs)
            pltpu.make_async_copy(
                joined_in.at[place, pl.ds(1, 2)], joined_in.at[place, pl.ds(1, 2)], out_recv.at[place]
            ).wait()
            pltpu.make_async_copy(joined_in.at[place, 0], joined_in.at[place, 0], query_recv.at[place]).wait()
        for t in range(3):
            for pair in range(pairs):
                joined_s[:, pair * LANES : (pair + 1) * LANES] = joined_in[pair, t]
            joined = joined_s[...]
            weight_load(t).wait()
            term = dot_nt(joined, weight_s[t % 2])
            grad_first[...] = term if t == 0 else grad_first[...] + term
            if t == 0:
                weight_load(2).start()
            if t != 1:
                row = 4 + t // 2
                late_s[row : row + 1] = jnp.sum(joined.astype(F32), 0, keepdims=True)

    def start_step():
        unit, inverse = normalised(start_ref[...])
        at_input, grad_gain, grad_shift = norm_backward(grad_first[...], gain_ref[...], unit, inverse)
        grad_start = at_input + grad_middle_ref[...]
        split = grad_start.reshape((2,) + own_tokens_ref.shape)
        tokens_s[...] = split.astype(BF16)
        tokens_copy().start()
        own_tokens_ref[...] = jnp.where(half == 0, split[0], split[1])
        lead = jnp.concatenate([lead_ref[...]] * (width // LANES), -1)
        late_s[0:1] = jnp.sum(lead * grad_start, 0, keepdims=True)
        late_s[1:2] = jnp.sum(grad_start, 0, keepdims=True)
        late_s[2:3] = grad_gain
        late_s[3:4] = grad_shift
        late_s[6:8] = jnp.zeros((2, width), F32)
        late.send()

    def near_step():
        near_copy().wait_recv()
        heads_near[...] = heads_near[...] + heads_in[:, :, own_rows]
        heads_flow.send()
        while heads_flow.at < len(heads_flow.stages):
            heads_flow.step()
        far_copy().start()

    def far_step():
        far_copy().wait_recv()
        heads_got[...] = heads_got[...] + heads_flow.held[half]

        @pl.when(lax.rem(me, copies) == 0)
        def _():
            for i, other in enumerate(others):
                heads_copy(i, other).start()
            heads_sum[me // copies] = heads_got[me]

    def members_step():
        for place in range(pairs):

            @pl.when(place * copies != me)
            def _():
                pltpu.make_async_copy(heads_sum.at[place], heads_sum.at[place], heads_recv.at[place]).wait()

        rows_copy().start()
        heads_rows[:, own_rows] = heads_sum[...]

    def rows_step():
        rows_copy().wait_recv()
        for pair in range(pairs):
            for t in range(3):
                column = t * width + pair * LANES
                heads_ref[:, column : column + LANES] = heads_rows[pair, :, t * LANES : (t + 1) * LANES]

    large = {
        "products": products_step, "joined": joined_step, "start": start_step, "near": near_step,
        "far": far_step, "members": members_step, "rows": rows_step,
    }
    for name, argument in rest:
        if name in large:
            large[name]()
        else:
            small_step(name, argument)
    late_ref[...] = late.held[...]
    early_ref[...] = early.held[...]

    for copy in grad_copies:
        copy.wait_send()
    for other in others:

        @pl.when(sends_to(other))
        def _():
            out_copy(other).wait_send()
            query_copy(other).wait_send()

    @pl.when(lax.rem(me, copies) == 0)
    def _():
        for i, other in enumerate(others):
            heads_copy(i, other).wait_send()

    for flow in flows + [late, early, heads_flow]:
        flow.drain()
    near_copy().wait_send()
    rows_copy().wait_send()
    far_copy().wait_send()
    for copy in first_copies:
        copy.wait_send()
    result_copy.wait()
    tokens_copy().wait()
    for k in range(count):
        for copy in gather_copies(k):
            copy.wait()


def backward(
    grad_blocks, qkv, key_aux, query, out_full, first, weight, start, grad_middle, gain, lead_rows,
    feed_vectors, up_vector, result, away, stay, plans, pairs, bands, grps, collective_id,
):
    members, _, block, _ = qkv.shape
    rows = members * block
    total, width = start.shape
    run = total // 2
    held = width // bands
    inner = up_vector.shape[1]
    arrays, count, grp_count = len(away), len(plans), bits(grps)
    z_low = bits(bands) - 2
    links = {("band", z_low): "z", ("band", z_low + 1): "Z"}
    links.update({("band", b): "x" for b in range(1, z_low)})
    links.update({("grp", b): "y" for b in range(grp_count)})
    vector_stages = [("band", b) for b in range(bits(bands))] + [("grp", b) for b in range(grp_count)]
    sizes = [2**bits(bands) * plan["rows"][1] * plan["columns"][1] / 2**20 for plan in plans]
    orders, steps, _, _ = plan_steps(sizes, links, vector_stages, members, 4.0 * rows / 2048, 7.0, 5.0)
    plans = [dict(plan, stages=order) for plan, order in zip(plans, orders)]
    shapes = [Flow.shapes(plan) for plan in plans]
    longest = max(len(plan["stages"]) for plan in plans)
    vmem = pl.BlockSpec(memory_space=pltpu.VMEM)
    anywhere = pl.BlockSpec(memory_space=pl.ANY)
    dma = pltpu.SemaphoreType.DMA
    return pl.pallas_call(
        functools.partial(backward_kernel, block, members, pairs, grps, plans, steps, vector_stages),
        out_shape=(
            jax.ShapeDtypeStruct((held, inner), BF16),
            jax.ShapeDtypeStruct((inner // bands, width), BF16),
            jax.ShapeDtypeStruct((held, width), BF16),
            jax.ShapeDtypeStruct((held, 3 * width), BF16),
            jax.ShapeDtypeStruct((8, width), F32),
            jax.ShapeDtypeStruct((8, width), F32),
            jax.ShapeDtypeStruct((run, width), F32),
            jax.ShapeDtypeStruct((run, width), BF16),
            jax.ShapeDtypeStruct((run, width), BF16),
            jax.ShapeDtypeStruct((len(first),) + first[0].shape, BF16),
        ),
        in_specs=[anywhere] + [vmem] * 4 + [anywhere] + [vmem] * 6 + [anywhere] * (1 + len(first) + 2 * arrays),
        out_specs=(anywhere, anywhere, anywhere, vmem, vmem, vmem, vmem, anywhere, anywhere, anywhere),
        scratch_shapes=[
            pltpu.VMEM((members, 1, block, LANES), BF16),
            pltpu.VMEM((2, rows, LANES), BF16),
            pltpu.VMEM((rows, LANES), BF16),
            pltpu.VMEM((rows, LANES), BF16),
            pltpu.VMEM((LANES, rows), F32),
            pltpu.VMEM((members, 3, block, LANES), BF16),
            pltpu.VMEM((pairs, 3, block, LANES), BF16),
            pltpu.VMEM((2, block, width), BF16),
            pltpu.VMEM((3 * LANES, width), F32),
            pltpu.VMEM((2, members, held, 3 * LANES), BF16),
            pltpu.VMEM((2, members, held // 2, 3 * LANES), BF16),
            pltpu.VMEM((members, held // 2, 3 * LANES), BF16),
            pltpu.VMEM((pairs, held // 2, 3 * LANES), BF16),
            pltpu.VMEM((pairs, held, 3 * LANES), BF16),
            pltpu.VMEM((2, width, width), BF16),
            pltpu.VMEM((total, width), BF16),
            pltpu.VMEM((2, run, width), BF16),
            pltpu.VMEM((8, width), F32),
            pltpu.VMEM((8, width), F32),
            pltpu.VMEM((total, width), F32),
        ]
        + [pltpu.VMEM(found[0], BF16) for found in shapes]
        + [pltpu.VMEM(found[1], BF16) for found in shapes]
        + [pltpu.VMEM(shape, BF16) for found in shapes for shape in found[1:]]
        + [pltpu.VMEM((8, width), F32) for _ in vector_stages * 2]
        + [pltpu.VMEM((2, members, held // 2, 3 * LANES), BF16) for _ in range(grp_count - 1)]
        + [
            dma, dma((members,)), dma((members,)), dma((members,)), dma((members,)), dma((members,)), dma((members,)),
            dma((len(first),)), dma((len(first),)), dma((2,)), dma((2,)), dma((2,)), dma((2,)),
            dma((len(vector_stages),)), dma((len(vector_stages),)), dma((len(vector_stages),)),
            dma((len(vector_stages),)), dma, dma,
            dma((members,)), dma((pairs,)), dma((grp_count,)), dma((grp_count,)),
            dma((count, grps)), dma((count, grps)), dma((count,)), dma, dma, dma, dma,
        ]
        + [dma((count,)), dma((count,)), dma((count,)), dma((count, longest)), dma((count, longest))],
        compiler_params=pltpu.CompilerParams(
            vmem_limit_bytes=62 * 2**20, collective_id=collective_id, has_side_effects=True
        ),
        cost_estimate=pl.CostEstimate(
            flops=24 * rows * rows * LANES, bytes_accessed=64 * 2**20, transcendentals=2 * rows * rows
        ),
        name="backward",
    )(
        grad_blocks, qkv, key_aux, query, out_full, weight, start, grad_middle, gain.reshape(1, width),
        lead_rows, feed_vectors, up_vector, result.reshape(2, run, width), *first, *away, *stay,
    )


SMALL_ROWS = (0, 1, 2, 3, 4, 5, 8, 9, 10, 11)


def emit_kernel(
    bands, up_ref, down_ref, output_ref, heads_ref, own_grads_ref, other_grads_ref, result_ref,
    other_result_ref, late_ref, early_ref,
    up_out, down_out, output_out, heads_out, grads_out, result_out, up_vector_out, *small_outs,
):
    band = lax.axis_index("band")
    held = late_ref.shape[1] // bands
    half = band // (bands // 2)
    up_out[...] = up_ref[...].astype(F32)
    down_out[...] = down_ref[...].astype(F32)
    output_out[...] = output_ref[...].astype(F32)
    heads_out[...] = heads_ref[...].astype(F32)
    own, other = own_grads_ref[...], other_grads_ref[...].astype(F32)
    grads_out[0] = jnp.where(half == 0, own, other)
    grads_out[1] = jnp.where(half == 0, other, own)
    other = other_result_ref[...]
    result_out[0] = jnp.where(half == 0, result_ref[0], other)
    result_out[1] = jnp.where(half == 0, other, result_ref[1])

    @pl.when(pl.program_id(0) == 0)
    def _():
        size = late_ref.shape[1] // bands
        here = pl.ds(pl.multiple_of(band * held // LANES * LANES, LANES), LANES)
        both = jnp.concatenate([late_ref[:, here], early_ref[:, here]], 0)
        value = both[:, :size]
        for i in range(1, LANES // size):
            value = jnp.where(lax.rem(band, LANES // size) == i, both[:, i * size : (i + 1) * size], value)
        for i, out in enumerate(small_outs):
            out[...] = value[SMALL_ROWS[i] : SMALL_ROWS[i] + 1]
        columns = up_vector_out.shape[1]
        spread = late_ref.shape[1] // columns
        at = pl.ds(pl.multiple_of(lax.rem(band, spread) * columns, columns), columns)
        value = early_ref[4:5, at]
        for i in range(1, 4):
            value = jnp.where(band // spread == i, early_ref[4 + i : 5 + i, at], value)
        up_vector_out[...] = value


def emit(up, down, output, heads, own_grads, other_grads, result, other_result, late, early, bands):
    run, width = own_grads.shape
    size = width // bands
    columns = 4 * width // bands
    steps = 2
    by_rows = lambda shape: pl.BlockSpec(
        shape[:-2] + (shape[-2] // steps, shape[-1]), lambda i: (0,) * (len(shape) - 2) + (i, 0)
    )
    matrices = (up, down, output, heads)
    both = (2, run, width)
    return pl.pallas_call(
        functools.partial(emit_kernel, bands),
        grid=(steps,),
            in_specs=[by_rows(m.shape) for m in matrices]
            + [by_rows((run, width)), by_rows((run, width)), by_rows(both), by_rows((run, width))]
            + [constant(8, width)] * 2,
            out_specs=tuple(by_rows(m.shape) for m in matrices)
            + (by_rows(both), by_rows(both), constant(1, columns))
            + (constant(1, size),) * len(SMALL_ROWS),
        out_shape=tuple(jax.ShapeDtypeStruct(m.shape, F32) for m in matrices)
        + (
            jax.ShapeDtypeStruct(both, F32),
            jax.ShapeDtypeStruct(both, BF16),
            jax.ShapeDtypeStruct((1, columns), F32),
        )
        + (jax.ShapeDtypeStruct((1, size), F32),) * len(SMALL_ROWS),
        compiler_params=pltpu.CompilerParams(vmem_limit_bytes=VMEM_BYTES),
        cost_estimate=pl.CostEstimate(flops=0, bytes_accessed=8 * 2**20, transcendentals=0),
        name="emit",
    )(
        up, down, output, heads, own_grads, other_grads,
        result.reshape(both), other_result, late, early,
    )


def swap(array, stage):
    axis, bit = stage
    size = lax.axis_size(axis)
    return lax.ppermute(array, axis, [(i, i ^ (1 << bit)) for i in range(size)])


def bit_of(stage):
    axis, bit = stage
    return (lax.axis_index(axis) >> bit) & 1


def take(array, axis, index):
    return lax.dynamic_index_in_dim(array, index, axis, keepdims=False)


def after(value, *others):
    return lax.optimization_barrier((value,) + others)[0]


def bits(size):
    return size.bit_length() - 1


def local(
    tokens,
    lead_index,
    segment,
    valid,
    lead_weight,
    lead_bias,
    first_gain,
    first_shift,
    heads_weight,
    query_bias,
    value_bias,
    output_weight,
    output_bias,
    second_gain,
    second_shift,
    up_weight,
    up_bias,
    down_weight,
    down_bias,
    cotangent,
):
    bands, grps = lax.axis_size("band"), lax.axis_size("grp")
    groups, rows, width = tokens.shape
    total = groups * rows
    pairs = width // LANES
    members = bands // groups
    band = lax.axis_index("band")
    far = ("band", bits(bands) - 1)
    own_group = bit_of(far)
    block = total

    core = lax.rem(band, 2).astype(jnp.int32).reshape(1)
    qkv, attended, grad_out, start, first_low, lead_rows, key_aux, out_full, query_marked = forward(
        tokens, cotangent, lead_index, segment, valid, lead_weight, lead_bias, first_gain, first_shift,
        heads_weight, query_bias, value_bias, members, 1,
    )

    def normed_of(offset):
        return lax.ppermute(
            after(first_low, attended), "band", [(i, i ^ offset) for i in range(bands)]
        )

    first_rows = [first_low] + [normed_of(2 * k) for k in range(1, members // 2)]

    (
        result, grad_middle, grad_blocks, down_away, down_stay, up_away, up_stay,
        output_away, output_stay, feed_vectors, grad_up_bias,
    ) = feed(
        core, attended, start, grad_out, output_weight, output_bias, second_gain, second_shift,
        up_weight, up_bias, down_weight, down_bias, bands,
    )
    split = lambda v: v.reshape((2,) * (bits(bands) - 1) + v.shape[1:])
    held_up, held_down, inner = up_stay.shape[1], down_stay.shape[1], up_weight.shape[1]
    lead = [b for b in range(1, bits(bands))][::-1]

    def plan(array, rows_of, columns_of):
        return {"array": array, "rows": rows_of, "columns": columns_of, "lead": lead}

    quarter, fourth = inner // 4, held_down // 4
    plans = []
    for i in range(4):
        plans.append(plan(0, (0, held_up), (i * quarter, quarter)))
        plans.append(plan(1, (i * fourth, fourth), (0, width)))
    plans.append(plan(2, (0, held_up), (0, width)))
    grad_up, grad_down, grad_output, grad_heads, late, early, own_grads, other_grads, other_result, _ = backward(
        grad_blocks, qkv, key_aux, query_marked, out_full, first_rows, heads_weight, start, grad_middle,
        first_gain, lead_rows, feed_vectors, grad_up_bias, result,
        [split(v) for v in (up_away, down_away, output_away)],
        [split(v) for v in (up_stay, down_stay, output_stay)],
        plans, pairs, bands, grps, 3,
    )
    grad_up, grad_down, grad_output, grad_heads, grad_tokens, outcome, *vectors = emit(
        grad_up, grad_down, grad_output, grad_heads, own_grads, other_grads, result, other_result,
        late, early, bands,
    )
    grad_up_bias, *small = [v.reshape(-1) for v in vectors]
    return (
        outcome,
        grad_tokens,
        *small[:4],
        grad_heads,
        *small[4:6],
        grad_output,
        *small[6:9],
        grad_up,
        grad_up_bias,
        grad_down,
        small[9],
    )


def solution(mesh):
    rows = P("grp", "band", None)
    in_specs = (rows, P("grp", None), P("grp", None), P("grp", None)) + (P(),) * 15 + (rows,)
    vector, matrix = P("band"), P("band", None)
    out_specs = (
        rows,
        rows,
        vector,
        vector,
        vector,
        vector,
        matrix,
        vector,
        vector,
        matrix,
        vector,
        vector,
        vector,
        matrix,
        vector,
        matrix,
        vector,
    )
    return jax.shard_map(local, mesh=mesh, in_specs=in_specs, out_specs=out_specs, check_vma=False)
```
